256 devices in a mesh: row: 32 (over x_hi, z, core), col: 8 (over x_lo, y).
Axes of the slice: x: 4 (x_hi: 2, x_lo: 2; x = x_hi * 2 + x_lo), y: 4, z: 8, core: 2. Of those that a mesh axis runs over, the one named last changes fastest.
Arguments:
- seqs: int32 [128, 4096], replicated, may hold values from 0 to 3
- fields: float32 [16384], replicated, may hold values from -4 to 320
- band: float32 [16384, 8704], P('row', 'col'), may hold values from -0.125 to 0.125, as said below
Outputs:
- new_band: float32 [16384, 8704], P('row', 'col')
- new_fields: float32 [16384], P(('row', 'col'))
The draws below stay inside these ranges and needn't reach their ends.
Inputs may be any that keep to these rules, and one draw needn't show every extreme that they name: band entries that are not live are zero, the tiles with j = 0 are symmetric, and entries whose row and column states belong to the same locus are zero.
All inputs are finite; a program needn't handle non-finite values.
Results may differ from the reference program's by a relative error of at most 0.0003.
Values sent between devices are 32-bit elements; how exact they have to be, the bound alone decides.
No kernel may reach another device: no remote copies, remote signals or barrier semaphores. Data moves between devices by JAX's collectives and lax.ppermute only.
A program may use at most 64 MiB of HBM per device.

```python
import jax
import jax.numpy as jnp
from jax import lax

L = 4096
Q = 4
B = 128
ROWB = 512
PIECE = 64
TILES = 17
BANDW = 8704
N_COL = 8


def draw_fields(key, part):
    key = jax.random.fold_in(key, 11)
    key_base = jax.random.fold_in(key, 0)
    values = jnp.clip(jax.random.normal(key_base, (L, Q), jnp.float32), -4.0, 4.0)
    return values.reshape(L * Q).astype(jnp.float32)


def draw_band(key, part):
    key = jax.random.fold_in(key, 23)
    state_count = L * Q
    block_count = state_count // ROWB
    shape = (block_count, ROWB, N_COL, TILES, PIECE)
    raw_values = jnp.clip(jax.random.normal(key, shape, jnp.float32), -4.0, 4.0)
    scaled = raw_values * (2.0 / L) ** 0.5
    diagonal = raw_values[:, :, :, 0, :].reshape(block_count, ROWB, ROWB)
    symmetric = (diagonal + jnp.swapaxes(diagonal, 1, 2)) * L ** (-0.5)
    locus_ids = jnp.arange(ROWB, dtype=jnp.int32) // Q
    symmetric = jnp.where(locus_ids[:, None] != locus_ids[None, :], symmetric, 0.0)
    scaled = scaled.at[:, :, :, 0, :].set(symmetric.reshape(block_count, ROWB, N_COL, PIECE))
    block_ids = jnp.arange(block_count, dtype=jnp.int32)[:, None, None, None, None]
    slot_ids = jnp.arange(TILES, dtype=jnp.int32)[None, None, None, :, None]
    dead = (slot_ids == block_count // 2) & (block_ids >= block_count // 2)
    return jnp.where(dead, 0.0, scaled).reshape(state_count, BANDW).astype(jnp.float32)


def place_ends(drawn, stream_key, least, largest):
    spot = [jax.random.randint(jax.random.fold_in(stream_key, axis), (), 0, length) for axis, length in enumerate(drawn.shape)]
    longest = drawn.shape.index(max(drawn.shape))
    beside = spot[:longest] + [(spot[longest] + 1) % drawn.shape[longest]] + spot[longest + 1:]
    return drawn.at[tuple(spot)].set(least).at[tuple(beside)].set(largest)


def setup_inputs(seed: int = 0) -> dict:
    splits = jax.random.split(jax.random.key(seed), 4)
    seqs = place_ends(jax.random.randint(splits[0], (B, L), 0, 4), jax.random.fold_in(splits[0], 1), 0, 3).astype(jnp.int32)
    fields = draw_fields(jax.random.fold_in(splits[3], 71), 0)
    band = draw_band(jax.random.fold_in(splits[3], 71), 0)
    return {"seqs": seqs, "fields": fields, "band": band}


step_rate = 1.0
coupling_decay = 0.25
field_decay = 0.1


def onehot_of(state_codes):
    table = state_codes[:, :, None] == jnp.arange(Q, dtype=jnp.int32)[None, None, :]
    return table.astype(jnp.float32).reshape(state_codes.shape[0], -1)


def residual_of(logits, onehot_part):
    batch_size = logits.shape[0]
    grouped = logits.reshape(batch_size, -1, Q)
    highest = jnp.max(grouped, axis=2, keepdims=True)
    expon = jnp.exp(grouped - highest)
    probabilities = expon / jnp.sum(expon, axis=2, keepdims=True)
    return onehot_part - probabilities.reshape(batch_size, -1)


def reference(seqs, fields, band):
    state_count = L * Q
    block_count = state_count // ROWB
    column_ids = jnp.arange(BANDW, dtype=jnp.int32)
    slot_ids = (column_ids // PIECE) % TILES
    piece_pos = (column_ids // (TILES * PIECE)) * PIECE + column_ids % PIECE
    onehot_all = onehot_of(seqs)
    band_blocks = band.reshape(block_count, ROWB, BANDW)
    block_ids = jnp.arange(block_count, dtype=jnp.int32)

    def columns_of(block_at):
        return (((block_at + slot_ids) % block_count) * ROWB + piece_pos).astype(jnp.int32)

    def live_of(block_at):
        dead = (slot_ids == block_count // 2) & (block_at >= block_count // 2)
        return jnp.where(dead, 0.0, 1.0).astype(jnp.float32)

    def logit_step(total, inputs):
        tile, block_at = inputs
        columns = columns_of(block_at)
        live = live_of(block_at)
        start = (block_at * ROWB).astype(jnp.int32)
        onehot_cols = jnp.take(onehot_all, columns, axis=1) * live[None, :]
        onehot_rows = lax.dynamic_slice_in_dim(onehot_all, start, ROWB, 1)
        row_part = lax.dot_general(onehot_cols, tile, (((1,), (1,)), ((), ())), precision=lax.Precision.HIGHEST, preferred_element_type=jnp.float32)
        routed = live * (slot_ids > 0).astype(jnp.float32)
        col_part = jnp.dot(onehot_rows, tile, precision=lax.Precision.HIGHEST, preferred_element_type=jnp.float32) * routed[None, :]
        total = total.at[:, columns].add(col_part)
        current = lax.dynamic_slice_in_dim(total, start, ROWB, 1)
        total = lax.dynamic_update_slice_in_dim(total, current + row_part, start, 1)
        return total, None

    total, _ = lax.scan(logit_step, jnp.zeros((B, state_count), jnp.float32), (band_blocks, block_ids))
    residual_all = residual_of(total + fields[None, :], onehot_all)

    def update_block(inputs):
        tile, block_at = inputs
        columns = columns_of(block_at)
        live = live_of(block_at)
        start = (block_at * ROWB).astype(jnp.int32)
        onehot_cols = jnp.take(onehot_all, columns, axis=1)
        resid_cols = jnp.take(residual_all, columns, axis=1)
        onehot_rows = lax.dynamic_slice_in_dim(onehot_all, start, ROWB, 1)
        resid_rows = lax.dynamic_slice_in_dim(residual_all, start, ROWB, 1)
        gradient = lax.dot_general(resid_rows, onehot_cols, (((0,), (0,)), ((), ())), precision=lax.Precision.HIGHEST, preferred_element_type=jnp.float32)
        gradient = gradient + lax.dot_general(onehot_rows, resid_cols, (((0,), (0,)), ((), ())), precision=lax.Precision.HIGHEST, preferred_element_type=jnp.float32)
        row_locus = (start + jnp.arange(ROWB, dtype=jnp.int32)) // Q
        col_locus = columns // Q
        keep_mask = live[None, :] * (row_locus[:, None] != col_locus[None, :]).astype(jnp.float32)
        return live[None, :] * (tile + step_rate * (keep_mask * (gradient / B) - coupling_decay * tile))

    new_band = lax.map(update_block, (band_blocks, block_ids)).reshape(state_count, BANDW)
    new_fields = fields + step_rate * (jnp.sum(residual_all, axis=0) / B - field_decay * fields)
    return new_band, new_fields
```

```python
import jax
import jax.numpy as jnp
from jax import lax
from jax.experimental import pallas as pl
from jax.experimental.pallas import tpu as pltpu
from jax.sharding import PartitionSpec as P

Q = 4
ROWS = 32
COLS = 8
HALF = 16
TILES = 17
PIECE = 64
LOCI = 16
SPAN = 512
BAND = TILES * PIECE
BATCH = 128
SENT = 3 * LOCI

step_rate = 1.0
coupling_decay = 0.25
field_decay = 0.1

LOW_GROUPS = [[h * HALF + l for l in range(HALF)] for h in range(2)]
SWAP_HALVES = [(i, i ^ HALF) for i in range(ROWS)]

f32 = jnp.float32
bf16 = jnp.bfloat16
NT = (((1,), (1,)), ((), ()))


def iota(shape, dim):
    return lax.broadcasted_iota(jnp.int32, shape, dim)


def split(x):
    hi = x.astype(bf16)
    return hi, (x - hi.astype(f32)).astype(bf16)


def mm(a, b):
    return jnp.dot(a, b, preferred_element_type=f32)


def seq_block(seqs_ref, at):
    start = pl.multiple_of(at * BATCH, BATCH)
    return seqs_ref[:, pl.ds(start, BATCH)].astype(f32).astype(bf16)


def logits_kernel(seqs_ref, band_ref, col_ref, last_ref, row_ref, codes_ref, hot, row_t, col_t):
    row_at = lax.axis_index("row")
    col_at = lax.axis_index("col")
    low_at = lax.rem(row_at, HALF)
    lane = iota((BATCH, 128), 1)
    pick = (iota((128, 128), 0) == col_at * LOCI + lane % PIECE // Q).astype(f32).astype(bf16)
    pick_loci = (
        (iota((LOCI, 128), 1) == col_at * LOCI + iota((LOCI, 128), 0)).astype(f32).astype(bf16)
    )
    spread = (iota((SPAN, 128), 1) == iota((SPAN, 128), 0) // Q).astype(f32).astype(bf16)
    state = (lane % Q).astype(f32)
    dead = row_at >= HALF
    own = None
    for pair in range(9):
        left = seq_block(seqs_ref, lax.rem(row_at + 2 * pair, ROWS))
        codes = mm(left, pick)
        if pair == 0:
            own = left
            codes_ref[0] = lax.dot_general(pick_loci, left, NT, preferred_element_type=f32)
        if pair < 8:
            right = seq_block(seqs_ref, lax.rem(row_at + 2 * pair + 1, ROWS))
            codes = jnp.where(lane < PIECE, codes, mm(right, pick))
        else:
            codes_ref[1] = lax.dot_general(pick_loci, left, NT, preferred_element_type=f32)
            codes = jnp.where((lane < PIECE) & jnp.logical_not(dead), codes, -1.0)
        hot[:, pair * 128 : pair * 128 + 128] = (codes == state).astype(f32).astype(bf16)
    codes_rows = lax.dot_general(spread, own, NT, preferred_element_type=f32)
    hot_rows = (codes_rows == (iota((SPAN, 128), 0) % Q).astype(f32)).astype(f32).astype(bf16)
    hi, lo = split(band_ref[...])
    col_t[...] = mm(hi, hot_rows) + mm(lo, hot_rows)
    part = mm(hot[:, :BAND], hi) + mm(hot[:, :BAND], lo)
    row_t[...] = part.T
    last = col_t[pl.ds(3, TILES * LOCI, stride=Q), :]
    last_row = row_t[pl.ds(3, COLS * LOCI, stride=Q), :]
    for a in range(3):
        diff = col_t[pl.ds(a, TILES * LOCI, stride=Q), :] - last
        place = slice(a * LOCI, (a + 1) * LOCI)
        col_ref[low_at, place, :] = jnp.zeros((LOCI, BATCH), f32)
        for j in range(1, HALF):
            to = lax.rem(low_at + j, HALF)
            col_ref[to, place, :] = diff[j * LOCI : (j + 1) * LOCI]
        last_ref[place, :] = jnp.where(dead, 0.0, diff[HALF * LOCI :])
        diff_row = row_t[pl.ds(a, COLS * LOCI, stride=Q), :] - last_row
        for c in range(COLS):
            row_ref[c, place, :] = diff_row[c * LOCI : (c + 1) * LOCI]


def hot_kernel(seqs_ref, hot_cols_ref, hot_rows_ref):
    row_at = lax.axis_index("row")
    col_at = lax.axis_index("col")
    pick = (
        (iota((PIECE, 128), 1) == col_at * LOCI + iota((PIECE, 128), 0) // Q)
        .astype(f32)
        .astype(bf16)
    )
    state = (iota((PIECE, 128), 0) % Q).astype(f32)
    for j in range(TILES):
        block = seq_block(seqs_ref, lax.rem(row_at + j, ROWS))
        codes = lax.dot_general(pick, block, NT, preferred_element_type=f32)
        hot_cols_ref[j * PIECE : (j + 1) * PIECE, :] = (codes == state).astype(f32).astype(bf16)
    own = seq_block(seqs_ref, row_at)
    spread = (iota((128, SPAN), 0) == iota((128, SPAN), 1) // Q).astype(f32).astype(bf16)
    codes = mm(own, spread)
    hot_rows_ref[...] = (
        (codes == (iota((BATCH, SPAN), 1) % Q).astype(f32)).astype(f32).astype(bf16)
    )


def sum_kernel(col_ref, last_ref, row_ref, out_ref):
    low_at = lax.rem(lax.axis_index("row"), HALF)
    own = row_ref[0]
    for c in range(1, COLS):
        own = own + row_ref[c]
    other = last_ref[...]
    for s in range(HALF):
        part = col_ref[s]
        own = own + jnp.where(s <= low_at, part, 0.0)
        other = other + jnp.where(s > low_at, part, 0.0)
    out_ref[:SENT, :] = own
    out_ref[SENT:, :] = other


def softmax_kernel(
    here_ref, there_ref, codes_ref, fields_ref, low_ref, row_ref, other_ref, new_fields_ref
):
    row_at = lax.axis_index("row")
    col_at = lax.axis_index("col")
    low_at = lax.rem(row_at, HALF)
    lane = iota((LOCI, 128), 1)
    locus = iota((LOCI, 128), 0)
    start = col_at % 2 * PIECE
    own = []
    other = []
    columns = []
    for block in range(2):
        block_at = lax.rem(row_at + block * HALF, ROWS)
        line = fields_ref[pl.ds(block_at * 4 + col_at // 2, 1), :]
        columns = [
            jnp.sum(jnp.where(lane == start + locus * Q + a, line, 0.0), axis=1, keepdims=True)
            for a in range(Q)
        ]
        if block == 0:
            own_columns = columns
        diffs = []
        for a in range(3):
            here = here_ref[block * SENT + a * LOCI : block * SENT + (a + 1) * LOCI, :]
            flip = (1 - block) * SENT + a * LOCI
            there = there_ref[flip : flip + LOCI, :]
            diffs.append(here + there + (columns[a] - columns[3]))
        highest = jnp.maximum(jnp.maximum(diffs[0], diffs[1]), jnp.maximum(diffs[2], 0.0))
        expon = [jnp.exp(d - highest) for d in diffs]
        total = expon[0] + expon[1] + expon[2] + jnp.exp(-highest)
        codes = codes_ref[block]
        resid = [
            jnp.where(codes == float(a), 1.0, 0.0) - expon[a] / total for a in range(3)
        ]
        if block == 0:
            own = resid
        else:
            other = resid
    sums = [jnp.sum(x, axis=1, keepdims=True) for x in own]
    sums.append(-(sums[0] + sums[1] + sums[2]))
    line = jnp.zeros((LOCI, 128), f32)
    for a in range(Q):
        value = own_columns[a] + step_rate * (sums[a] / BATCH - field_decay * own_columns[a])
        line = line + jnp.where(lane == locus * Q + a, value, 0.0)
    new_fields_ref[...] = jnp.sum(line, axis=0, keepdims=True)
    for a in range(3):
        place = slice(a * LOCI, (a + 1) * LOCI)
        other_ref[place, :] = other[a]
        for c in range(COLS):
            row_ref[c, place, :] = own[a]
        for s in range(HALF):
            low_ref[s, place, :] = jnp.where(low_at >= s, own[a], other[a])


def update_kernel(
    band_ref, low_ref, other_ref, row_ref, hot_cols_ref, hot_rows_ref, out_ref, rows, cols
):
    row_at = lax.axis_index("row")
    col_at = lax.axis_index("col")
    low_at = lax.rem(row_at, HALF)
    for j in range(TILES):
        if j < HALF:
            part = low_ref[lax.rem(low_at + j, HALF)]
        else:
            part = other_ref[...]
        pieces = [part[a * LOCI : (a + 1) * LOCI] for a in range(3)]
        pieces.append(-(pieces[0] + pieces[1] + pieces[2]))
        for a in range(Q):
            cols[pl.ds(j * PIECE + a, LOCI, stride=Q), :] = pieces[a]
    for c in range(COLS):
        pieces = [row_ref[c, a * LOCI : (a + 1) * LOCI, :] for a in range(3)]
        pieces.append(-(pieces[0] + pieces[1] + pieces[2]))
        for a in range(Q):
            rows[pl.ds(c * PIECE + a, LOCI, stride=Q), :] = pieces[a]
    rows_hi, rows_lo = split(rows[...].T)
    right = jnp.concatenate([rows_hi, rows_lo, hot_rows_ref[...], hot_rows_ref[...]], axis=0)
    dead = row_at >= HALF
    for chunk in range(4):
        at = slice(chunk * 272, (chunk + 1) * 272)
        cols_hi, cols_lo = split(cols[at, :])
        hot = hot_cols_ref[at, :]
        gradient = mm(jnp.concatenate([hot, hot, cols_hi, cols_lo], axis=1), right)
        band = band_ref[at, :]
        spot = iota((272, SPAN), 0) + chunk * 272
        if chunk == 0:
            same = (spot < PIECE) & (
                (col_at * PIECE + spot) // Q == iota((272, SPAN), 1) // Q
            )
            gradient = jnp.where(same, 0.0, gradient)
        new = band + step_rate * (gradient / BATCH - coupling_decay * band)
        if chunk == 3:
            new = jnp.where(dead & (spot >= HALF * PIECE), 0.0, new)
        out_ref[at, :] = new


def call(kernel, outs, scratch=(), name=None):
    return pl.pallas_call(
        kernel,
        out_shape=outs,
        scratch_shapes=list(scratch),
        compiler_params=pltpu.CompilerParams(vmem_limit_bytes=48 * 1024 * 1024),
        name=name,
    )


def arr(*shape, dtype=f32):
    return jax.ShapeDtypeStruct(shape, dtype)


def shards(seqs, fields, band):
    band_t = band.T
    col_send, last, row_send, codes = call(
        logits_kernel,
        (
            arr(HALF, SENT, BATCH),
            arr(SENT, BATCH),
            arr(COLS, SENT, BATCH),
            arr(2, LOCI, BATCH),
        ),
        [
            pltpu.VMEM((BATCH, 9 * 128), bf16),
            pltpu.VMEM((SPAN, BATCH), f32),
            pltpu.VMEM((BAND, BATCH), f32),
        ],
        "logit_parts",
    )(seqs, band_t)
    row_got = lax.all_to_all(row_send, "col", 0, 0, tiled=True)
    col_got = lax.all_to_all(col_send, "row", 0, 0, tiled=True, axis_index_groups=LOW_GROUPS)
    hot_cols, hot_rows = call(
        hot_kernel, (arr(BAND, BATCH, dtype=bf16), arr(BATCH, SPAN, dtype=bf16)), name="one_hots"
    )(seqs)
    here = call(sum_kernel, arr(2 * SENT, BATCH), name="sum_parts")(col_got, last, row_got)
    there = lax.ppermute(here, "row", SWAP_HALVES)
    low_send, row_resid, other, new_fields = call(
        softmax_kernel,
        (
            arr(HALF, SENT, BATCH),
            arr(COLS, SENT, BATCH),
            arr(SENT, BATCH),
            arr(1, 128),
        ),
        name="softmax",
    )(here, there, codes, fields.reshape(-1, 128))
    row_all = lax.all_to_all(row_resid, "col", 0, 0, tiled=True)
    low_all = lax.all_to_all(low_send, "row", 0, 0, tiled=True, axis_index_groups=LOW_GROUPS)
    new_band_t = call(
        update_kernel,
        arr(BAND, SPAN),
        [pltpu.VMEM((SPAN, BATCH), f32), pltpu.VMEM((BAND, BATCH), f32)],
        "update",
    )(band_t, low_all, other, row_all, hot_cols, hot_rows)
    return new_band_t.T, new_fields[0, :PIECE]


def solution(mesh):
    in_specs = (P(), P(), P("row", "col"))
    out_specs = (P("row", "col"), P(("row", "col")))
    return jax.shard_map(shards, mesh=mesh, in_specs=in_specs, out_specs=out_specs, check_vma=False)
```

```python
import jax
import jax.numpy as jnp
from jax import lax
from jax.experimental import pallas as pl
from jax.experimental.pallas import tpu as pltpu
from jax.sharding import PartitionSpec as P

Q = 4
ROWS = 32
COLS = 8
HALF = 16
TILES = 17
PIECE = 64
LOCI = 16
SPAN = 512
BAND = TILES * PIECE
BATCH = 128
SENT = 3 * LOCI

step_rate = 1.0
coupling_decay = 0.25
field_decay = 0.1

DEPTH = 8
Z_GROUPS = [[(h * DEPTH + z) * 2 + k for z in range(DEPTH)] for h in range(2) for k in range(2)]
SWAP_CORES = [(i, i ^ 1) for i in range(ROWS)]
SWAP_HALVES = [(i, i ^ HALF) for i in range(ROWS)]


def swap_cols(x, step):
    return lax.ppermute(x, "col", [(i, i ^ step) for i in range(COLS)])


NEAR = 4
CHUNKS = [slice(0, 256), slice(256, 512), slice(512, 768), slice(768, BAND)]

f32 = jnp.float32
bf16 = jnp.bfloat16
NT = (((1,), (1,)), ((), ()))


def iota(shape, dim):
    return lax.broadcasted_iota(jnp.int32, shape, dim)


def split(x):
    hi = x.astype(bf16)
    return hi, (x - hi.astype(f32)).astype(bf16)


def mm(a, b):
    return jnp.dot(a, b, preferred_element_type=f32)


def logits_kernel(
    seqs_ref,
    band_ref,
    codes_ref,
    mine_ref,
    core_ref,
    keep_ref,
    give_ref,
    hot,
    hot_rows_ref,
    blocks,
    band,
    row_t,
    col_t,
    block_sems,
    band_sems,
):
    row_at = lax.axis_index("row")
    col_at = lax.axis_index("col")
    block_copies = []
    for j in range(TILES):
        start = pl.multiple_of(lax.rem(row_at + j, ROWS) * BATCH, BATCH)
        block_copies.append(
            pltpu.make_async_copy(
                seqs_ref.at[:, pl.ds(start, BATCH)], blocks.at[j], block_sems.at[j]
            )
        )
    band_copies = [
        pltpu.make_async_copy(band_ref.at[at], band.at[at], band_sems.at[i])
        for i, at in enumerate(CHUNKS)
    ]
    for copy in block_copies + band_copies:
        copy.start()
    lane = iota((BATCH, 128), 1)
    pick = (iota((128, 128), 0) == col_at * LOCI + lane % PIECE // Q).astype(f32).astype(bf16)
    pick_loci = (
        (iota((LOCI, 128), 1) == col_at * LOCI + iota((LOCI, 128), 0)).astype(f32).astype(bf16)
    )
    spread = (iota((SPAN, 128), 1) == iota((SPAN, 128), 0) // Q).astype(f32).astype(bf16)
    state = (lane % Q).astype(f32)
    dead = row_at >= HALF

    for copy in block_copies:
        copy.wait()

    def block(j):
        return blocks[j].astype(f32).astype(bf16)

    own = block(0)
    codes_ref[0] = lax.dot_general(pick_loci, own, NT, preferred_element_type=f32)
    codes_rows = lax.dot_general(spread, own, NT, preferred_element_type=f32)
    hot_rows = (codes_rows == (iota((SPAN, 128), 0) % Q).astype(f32)).astype(f32).astype(bf16)
    hot_rows_ref[...] = hot_rows
    for pair in range(9):
        left = block(2 * pair) if pair else own
        codes = mm(left, pick)
        if pair < 8:
            codes = jnp.where(lane < PIECE, codes, mm(block(2 * pair + 1), pick))
        else:
            codes_ref[1] = lax.dot_general(pick_loci, left, NT, preferred_element_type=f32)
            codes = jnp.where((lane < PIECE) & jnp.logical_not(dead), codes, -1.0)
        hot[:, pair * 128 : pair * 128 + 128] = (codes == state).astype(f32).astype(bf16)
    part = None
    for chunk, at in enumerate(CHUNKS):
        if chunk % 2 == 0:
            band_copies[chunk].wait()
            band_copies[chunk + 1].wait()
        hi, lo = split(band[at, :])
        col_t[at, :] = mm(hi, hot_rows) + mm(lo, hot_rows)
        term = mm(hot[:, at], hi) + mm(hot[:, at], lo)
        part = term if part is None else part + term
    row_t[...] = part.T
    last = col_t[pl.ds(3, TILES * LOCI, stride=Q), :]
    for a in range(3):
        diff = col_t[pl.ds(a, TILES * LOCI, stride=Q), :] - last
        place = slice(a * LOCI, (a + 1) * LOCI)
        for e in range(DEPTH):
            core_ref[e, place, :] = diff[(2 * e + 1) * LOCI : (2 * e + 2) * LOCI]
            value = diff[(2 * e + 2) * LOCI : (2 * e + 3) * LOCI]
            if e == DEPTH - 1:
                value = jnp.where(dead, 0.0, value)
            mine_ref[e, place, :] = value
    for step in range(COLS):
        start = (col_at ^ step) * PIECE
        to = keep_ref if step < NEAR else give_ref
        last = row_t[pl.ds(start + 3, LOCI, stride=Q), :]
        for a in range(3):
            place = slice(a * LOCI, (a + 1) * LOCI)
            to[step % NEAR, place, :] = row_t[pl.ds(start + a, LOCI, stride=Q), :] - last


def place_of():
    row_at = lax.axis_index("row")
    return row_at, lax.rem(row_at, 2) == 1, lax.rem(row_at // 2, DEPTH)


def combine_kernel(mine_ref, core_ref, keep_ref, got_ref, z_ref, last_ref, *part_refs):
    _, odd, z_at = place_of()
    for d in range(DEPTH + 1):
        lower = core_ref[d] if d < DEPTH else jnp.zeros((SENT, BATCH), f32)
        upper = core_ref[d - 1] if d else jnp.zeros((SENT, BATCH), f32)
        value = jnp.where(odd, lower, upper)
        if d:
            value = value + mine_ref[d - 1]
        if d < DEPTH:
            z_ref[lax.rem(z_at + d, DEPTH)] = value
        else:
            last_ref[...] = value
    for step in range(NEAR):
        part_refs[step][...] = keep_ref[step] + got_ref[step]


def sum_kernel(z_ref, last_ref, *rest):
    row_refs, out_ref = rest[:NEAR], rest[NEAR]
    _, _, z_at = place_of()
    own = row_refs[0][...]
    for step in range(1, NEAR):
        own = own + row_refs[step][...]
    other = last_ref[...]
    for s in range(DEPTH):
        part = z_ref[s]
        own = own + jnp.where(s <= z_at, part, 0.0)
        other = other + jnp.where(s > z_at, part, 0.0)
    out_ref[:SENT, :] = own
    out_ref[SENT:, :] = other


def choose_kernel(z_ref, other_ref, core_ref):
    _, odd, z_at = place_of()
    for e in range(DEPTH):
        lower = z_ref[lax.rem(z_at + e, DEPTH)]
        upper = z_ref[lax.rem(z_at + e + 1, DEPTH)] if e < DEPTH - 1 else other_ref[...]
        core_ref[e] = jnp.where(odd, lower, upper)


def flip_kernel(hot_ref, hot_rows_ref, hot_t_ref, hot_rows_t_ref):
    eye = (iota((128, 128), 0) == iota((128, 128), 1)).astype(f32).astype(bf16)
    for j in range(9):
        at = slice(j * 128, min(BAND, (j + 1) * 128))
        turned = lax.dot_general(
            hot_ref[:, at], eye, (((0,), (0,)), ((), ())), preferred_element_type=f32
        )
        hot_t_ref[at, :] = turned.astype(bf16)
    turned = lax.dot_general(eye, hot_rows_ref[...], NT, preferred_element_type=f32)
    hot_rows_t_ref[...] = turned.astype(bf16)


def pair_kernel(own_ref, got_ref, out_ref):
    out_ref[0] = own_ref[...]
    out_ref[1] = got_ref[...]


def softmax_kernel(
    here_ref, there_ref, codes_ref, fields_ref, z_ref, row_ref, other_ref, new_fields_ref
):
    row_at = lax.axis_index("row")
    col_at = lax.axis_index("col")
    z_at = lax.rem(row_at // 2, DEPTH)
    lane = iota((LOCI, 128), 1)
    locus = iota((LOCI, 128), 0)
    start = col_at % 2 * PIECE
    own = []
    other = []
    columns = []
    for block in range(2):
        block_at = lax.rem(row_at + block * HALF, ROWS)
        line = fields_ref[pl.ds(block_at * 4 + col_at // 2, 1), :]
        columns = [
            jnp.sum(jnp.where(lane == start + locus * Q + a, line, 0.0), axis=1, keepdims=True)
            for a in range(Q)
        ]
        if block == 0:
            own_columns = columns
        diffs = []
        for a in range(3):
            here = here_ref[block * SENT + a * LOCI : block * SENT + (a + 1) * LOCI, :]
            flip = (1 - block) * SENT + a * LOCI
            there = there_ref[flip : flip + LOCI, :]
            diffs.append(here + there + (columns[a] - columns[3]))
        highest = jnp.maximum(jnp.maximum(diffs[0], diffs[1]), jnp.maximum(diffs[2], 0.0))
        expon = [jnp.exp(d - highest) for d in diffs]
        total = expon[0] + expon[1] + expon[2] + jnp.exp(-highest)
        codes = codes_ref[block]
        resid = [
            jnp.where(codes == float(a), 1.0, 0.0) - expon[a] / total for a in range(3)
        ]
        if block == 0:
            own = resid
        else:
            other = resid
    sums = [jnp.sum(x, axis=1, keepdims=True) for x in own]
    sums.append(-(sums[0] + sums[1] + sums[2]))
    line = jnp.zeros((LOCI, 128), f32)
    for a in range(Q):
        value = own_columns[a] + step_rate * (sums[a] / BATCH - field_decay * own_columns[a])
        line = line + jnp.where(lane == locus * Q + a, value, 0.0)
    new_fields_ref[...] = jnp.sum(line, axis=0, keepdims=True)
    for a in range(3):
        place = slice(a * LOCI, (a + 1) * LOCI)
        other_ref[place, :] = other[a]
        row_ref[place, :] = own[a]
        for s in range(DEPTH):
            z_ref[s, place, :] = jnp.where(z_at >= s, own[a], other[a])


def update_kernel(band_ref, z_ref, other_ref, core_ref, hot_cols_ref, hot_rows_ref, *rest):
    row_refs, (out_ref, rows, cols, new_ref, sems) = rest[:NEAR], rest[NEAR:]
    row_at = lax.axis_index("row")
    col_at = lax.axis_index("col")
    z_at = lax.rem(row_at // 2, DEPTH)
    for j in range(TILES):
        if j % 2:
            part = core_ref[j // 2]
        elif j < HALF:
            part = z_ref[lax.rem(z_at + j // 2, DEPTH)]
        else:
            part = other_ref[...]
        pieces = [part[a * LOCI : (a + 1) * LOCI] for a in range(3)]
        pieces.append(-(pieces[0] + pieces[1] + pieces[2]))
        for a in range(Q):
            cols[pl.ds(j * PIECE + a, LOCI, stride=Q), :] = pieces[a]
    for step in range(COLS):
        part = row_refs[step % NEAR][step // NEAR]
        pieces = [part[a * LOCI : (a + 1) * LOCI, :] for a in range(3)]
        pieces.append(-(pieces[0] + pieces[1] + pieces[2]))
        for a in range(Q):
            at = (col_at ^ step) * PIECE + a
            rows[pl.ds(at, LOCI, stride=Q), :] = pieces[a]
    rows_hi, rows_lo = split(rows[...].T)
    right = jnp.concatenate([rows_hi, rows_lo, hot_rows_ref[...], hot_rows_ref[...]], axis=0)
    dead = row_at >= HALF
    copies = []
    for chunk, at in enumerate(CHUNKS):
        cols_hi, cols_lo = split(cols[at, :])
        hot = hot_cols_ref[at, :]
        gradient = mm(jnp.concatenate([hot, hot, cols_hi, cols_lo], axis=1), right)
        band = band_ref[at, :]
        spot = iota(band.shape, 0) + at.start
        if chunk == 0:
            same = (spot < PIECE) & ((col_at * PIECE + spot) // Q == iota(band.shape, 1) // Q)
            gradient = jnp.where(same, 0.0, gradient)
        new = band + step_rate * (gradient / BATCH - coupling_decay * band)
        if chunk == len(CHUNKS) - 1:
            new = jnp.where(dead & (spot >= HALF * PIECE), 0.0, new)
        new_ref[at, :] = new
        copies.append(pltpu.make_async_copy(new_ref.at[at], out_ref.at[at], sems.at[chunk]))
        copies[-1].start()
    for copy in copies:
        copy.wait()


def call(kernel, outs, scratch=(), name=None, hbm=False, hbm_out=False):
    specs = {"in_specs": [pl.BlockSpec(memory_space=pltpu.HBM)] * 2} if hbm else {}
    if hbm_out:
        specs["out_specs"] = pl.BlockSpec(memory_space=pltpu.HBM)
    return pl.pallas_call(
        kernel,
        out_shape=outs,
        scratch_shapes=list(scratch),
        compiler_params=pltpu.CompilerParams(
            vmem_limit_bytes=(52 if hbm else 24) * 1024 * 1024
        ),
        name=name,
        **specs,
    )


def arr(*shape, dtype=f32):
    return jax.ShapeDtypeStruct(shape, dtype)


def shards(seqs, fields, band):
    band_t = band.T
    piece = arr(SENT, BATCH)
    four = arr(NEAR, SENT, BATCH)
    eight = arr(DEPTH, SENT, BATCH)
    codes, mine, core, keep, give, hot, hot_rows = call(
        logits_kernel,
        (
            arr(2, LOCI, BATCH),
            eight,
            eight,
            four,
            four,
            arr(BATCH, 9 * 128, dtype=bf16),
            arr(SPAN, BATCH, dtype=bf16),
        ),
        [
            pltpu.VMEM((TILES, BATCH, 128), jnp.int32),
            pltpu.VMEM((BAND, SPAN), f32),
            pltpu.VMEM((SPAN, BATCH), f32),
            pltpu.VMEM((BAND, BATCH), f32),
            pltpu.SemaphoreType.DMA((TILES,)),
            pltpu.SemaphoreType.DMA((len(CHUNKS),)),
        ],
        "logit_parts",
        hbm=True,
    )(seqs, band_t)
    core = lax.ppermute(core, "row", SWAP_CORES)
    give = swap_cols(give, NEAR)
    z_send, last, *parts = call(
        combine_kernel, (eight, piece) + (piece,) * NEAR, name="combine"
    )(mine, core, keep, give)
    z_got = lax.all_to_all(z_send, "row", 0, 0, tiled=True, axis_index_groups=Z_GROUPS)
    row_got = [parts[0]] + [swap_cols(parts[step], step) for step in range(1, NEAR)]
    hot_cols, hot_rows = call(
        flip_kernel, (arr(BAND, BATCH, dtype=bf16), arr(BATCH, SPAN, dtype=bf16)), name="flip"
    )(hot, hot_rows)
    here = call(sum_kernel, arr(2 * SENT, BATCH), name="sum_parts")(z_got, last, *row_got)
    there = lax.ppermute(here, "row", SWAP_HALVES)
    z_send, resid, other, new_fields = call(
        softmax_kernel,
        (eight, piece, piece, arr(1, 128)),
        name="softmax",
    )(here, there, codes, fields.reshape(-1, 128))
    across = swap_cols(resid, NEAR)
    z_all = lax.all_to_all(z_send, "row", 0, 0, tiled=True, axis_index_groups=Z_GROUPS)
    pair = call(pair_kernel, arr(2, SENT, BATCH), name="pair")(resid, across)
    row_all = [pair] + [swap_cols(pair, step) for step in range(1, NEAR)]
    core_all = lax.ppermute(
        call(choose_kernel, eight, name="choose")(z_all, other), "row", SWAP_CORES
    )
    new_band_t = call(
        update_kernel,
        arr(BAND, SPAN),
        [
            pltpu.VMEM((SPAN, BATCH), f32),
            pltpu.VMEM((BAND, BATCH), f32),
            pltpu.VMEM((BAND, SPAN), f32),
            pltpu.SemaphoreType.DMA((len(CHUNKS),)),
        ],
        "update",
        hbm_out=True,
    )(band_t, z_all, other, core_all, hot_cols, hot_rows, *row_all)
    return new_band_t.T, new_fields[0, :PIECE]


def solution(mesh):
    in_specs = (P(), P(), P("row", "col"))
    out_specs = (P("row", "col"), P(("row", "col")))
    return jax.shard_map(shards, mesh=mesh, in_specs=in_specs, out_specs=out_specs, check_vma=False)
```

```python
import jax
import jax.numpy as jnp
from jax import lax
from jax.experimental import pallas as pl
from jax.experimental.pallas import tpu as pltpu
from jax.sharding import PartitionSpec as P

Q = 4
ROWS = 32
COLS = 8
HALF = 16
TILES = 17
PIECE = 64
LOCI = 16
SPAN = 512
BAND = TILES * PIECE
BATCH = 128
SENT = 3 * LOCI

step_rate = 1.0
coupling_decay = 0.25
field_decay = 0.1

DEPTH = 8
PLANES = [7, 6, 5, 4, 0, 1, 2, 3]
Z_GROUPS = [[(h * DEPTH + z) * 2 + k for z in PLANES] for h in range(2) for k in range(2)]
SWAP_CORES = [(i, i ^ 1) for i in range(ROWS)]
SWAP_HALVES = [(i, i ^ HALF) for i in range(ROWS)]


def swap_cols(x, step):
    return lax.ppermute(x, "col", [(i, i ^ step) for i in range(COLS)])


NEAR = 4
CHUNKS = [slice(0, 256), slice(256, 512), slice(512, 768), slice(768, BAND)]

f32 = jnp.float32
bf16 = jnp.bfloat16
NT = (((1,), (1,)), ((), ()))


def iota(shape, dim):
    return lax.broadcasted_iota(jnp.int32, shape, dim)


def split(x):
    hi = x.astype(bf16)
    return hi, (x - hi.astype(f32)).astype(bf16)


def mm(a, b):
    return jnp.dot(a, b, preferred_element_type=f32)


def logits_kernel(
    seqs_ref,
    band_ref,
    codes_ref,
    mine_ref,
    core_ref,
    keep_ref,
    give_ref,
    hot,
    hot_rows_ref,
    blocks,
    band,
    row_t,
    col_t,
    block_sems,
    band_sems,
):
    row_at = lax.axis_index("row")
    col_at = lax.axis_index("col")
    block_copies = []
    for j in range(TILES):
        start = pl.multiple_of(lax.rem(row_at + j, ROWS) * BATCH, BATCH)
        block_copies.append(
            pltpu.make_async_copy(
                seqs_ref.at[:, pl.ds(start, BATCH)], blocks.at[j], block_sems.at[j]
            )
        )
    band_copies = [
        pltpu.make_async_copy(band_ref.at[at], band.at[at], band_sems.at[i])
        for i, at in enumerate(CHUNKS)
    ]
    for copy in block_copies + band_copies:
        copy.start()
    lane = iota((BATCH, 128), 1)
    pick = (iota((128, 128), 0) == col_at * LOCI + lane % PIECE // Q).astype(f32).astype(bf16)
    pick_loci = (
        (iota((LOCI, 128), 1) == col_at * LOCI + iota((LOCI, 128), 0)).astype(f32).astype(bf16)
    )
    spread = (iota((SPAN, 128), 1) == iota((SPAN, 128), 0) // Q).astype(f32).astype(bf16)
    state = (lane % Q).astype(f32)
    dead = row_at >= HALF

    for copy in block_copies:
        copy.wait()

    def block(j):
        return blocks[j].astype(f32).astype(bf16)

    own = block(0)
    codes_ref[0] = lax.dot_general(pick_loci, own, NT, preferred_element_type=f32)
    codes_rows = lax.dot_general(spread, own, NT, preferred_element_type=f32)
    hot_rows = (codes_rows == (iota((SPAN, 128), 0) % Q).astype(f32)).astype(f32).astype(bf16)
    hot_rows_ref[...] = hot_rows
    for pair in range(9):
        left = block(2 * pair) if pair else own
        codes = mm(left, pick)
        if pair < 8:
            codes = jnp.where(lane < PIECE, codes, mm(block(2 * pair + 1), pick))
        else:
            codes_ref[1] = lax.dot_general(pick_loci, left, NT, preferred_element_type=f32)
            codes = jnp.where((lane < PIECE) & jnp.logical_not(dead), codes, -1.0)
        hot[:, pair * 128 : pair * 128 + 128] = (codes == state).astype(f32).astype(bf16)
    part = None
    for chunk, at in enumerate(CHUNKS):
        if chunk % 2 == 0:
            band_copies[chunk].wait()
            band_copies[chunk + 1].wait()
        hi, lo = split(band[at, :])
        col_t[at, :] = mm(hi, hot_rows) + mm(lo, hot_rows)
        term = mm(hot[:, at], hi) + mm(hot[:, at], lo)
        part = term if part is None else part + term
    row_t[...] = part.T
    last = col_t[pl.ds(3, TILES * LOCI, stride=Q), :]
    for a in range(3):
        diff = col_t[pl.ds(a, TILES * LOCI, stride=Q), :] - last
        place = slice(a * LOCI, (a + 1) * LOCI)
        for e in range(DEPTH):
            core_ref[e, place, :] = diff[(2 * e + 1) * LOCI : (2 * e + 2) * LOCI]
            value = diff[(2 * e + 2) * LOCI : (2 * e + 3) * LOCI]
            if e == DEPTH - 1:
                value = jnp.where(dead, 0.0, value)
            mine_ref[e, place, :] = value
    for step in range(COLS):
        start = (col_at ^ step) * PIECE
        to = keep_ref if step < NEAR else give_ref
        last = row_t[pl.ds(start + 3, LOCI, stride=Q), :]
        for a in range(3):
            place = slice(a * LOCI, (a + 1) * LOCI)
            to[step % NEAR, place, :] = row_t[pl.ds(start + a, LOCI, stride=Q), :] - last


def slot_of(z):
    z = lax.rem(z, DEPTH)
    return jnp.where(z < 4, z + 4, 7 - z)


def place_of():
    row_at = lax.axis_index("row")
    return row_at, lax.rem(row_at, 2) == 1, lax.rem(row_at // 2, DEPTH)


def combine_kernel(mine_ref, core_ref, keep_ref, got_ref, z_ref, last_ref, *part_refs):
    _, odd, z_at = place_of()
    for d in range(DEPTH + 1):
        lower = core_ref[d] if d < DEPTH else jnp.zeros((SENT, BATCH), f32)
        upper = core_ref[d - 1] if d else jnp.zeros((SENT, BATCH), f32)
        value = jnp.where(odd, lower, upper)
        if d:
            value = value + mine_ref[d - 1]
        if d < DEPTH:
            z_ref[slot_of(z_at + d)] = value
        else:
            last_ref[...] = value
    for step in range(NEAR):
        part_refs[step][...] = keep_ref[step] + got_ref[step]


def sum_kernel(z_ref, last_ref, hot_ref, hot_rows_ref, *rest):
    del hot_ref, hot_rows_ref
    row_refs, out_ref = rest[:NEAR], rest[NEAR]
    _, _, z_at = place_of()
    own = row_refs[0][...]
    for step in range(1, NEAR):
        own = own + row_refs[step][...]
    other = last_ref[...]
    for s in range(DEPTH):
        part = z_ref[PLANES.index(s)]
        own = own + jnp.where(s <= z_at, part, 0.0)
        other = other + jnp.where(s > z_at, part, 0.0)
    out_ref[:SENT, :] = own
    out_ref[SENT:, :] = other


def choose_kernel(z_ref, other_ref, core_ref):
    _, odd, z_at = place_of()
    for e in range(DEPTH):
        lower = z_ref[slot_of(z_at + e)]
        upper = z_ref[slot_of(z_at + e + 1)] if e < DEPTH - 1 else other_ref[...]
        core_ref[e] = jnp.where(odd, lower, upper)


def flip_kernel(hot_ref, hot_rows_ref, hot_t_ref, hot_rows_t_ref):
    eye = (iota((128, 128), 0) == iota((128, 128), 1)).astype(f32).astype(bf16)
    for j in range(9):
        at = slice(j * 128, min(BAND, (j + 1) * 128))
        turned = lax.dot_general(
            hot_ref[:, at], eye, (((0,), (0,)), ((), ())), preferred_element_type=f32
        )
        hot_t_ref[at, :] = turned.astype(bf16)
    turned = lax.dot_general(eye, hot_rows_ref[...], NT, preferred_element_type=f32)
    hot_rows_t_ref[...] = turned.astype(bf16)


def pair_kernel(own_ref, got_ref, out_ref):
    out_ref[0] = own_ref[...]
    out_ref[1] = got_ref[...]


def softmax_kernel(
    here_ref, there_ref, codes_ref, fields_ref, z_ref, row_ref, other_ref, new_fields_ref
):
    row_at = lax.axis_index("row")
    col_at = lax.axis_index("col")
    z_at = lax.rem(row_at // 2, DEPTH)
    lane = iota((LOCI, 128), 1)
    locus = iota((LOCI, 128), 0)
    start = col_at % 2 * PIECE
    own = []
    other = []
    columns = []
    for block in range(2):
        block_at = lax.rem(row_at + block * HALF, ROWS)
        line = fields_ref[pl.ds(block_at * 4 + col_at // 2, 1), :]
        columns = [
            jnp.sum(jnp.where(lane == start + locus * Q + a, line, 0.0), axis=1, keepdims=True)
            for a in range(Q)
        ]
        if block == 0:
            own_columns = columns
        diffs = []
        for a in range(3):
            here = here_ref[block * SENT + a * LOCI : block * SENT + (a + 1) * LOCI, :]
            flip = (1 - block) * SENT + a * LOCI
            there = there_ref[flip : flip + LOCI, :]
            diffs.append(here + there + (columns[a] - columns[3]))
        highest = jnp.maximum(jnp.maximum(diffs[0], diffs[1]), jnp.maximum(diffs[2], 0.0))
        expon = [jnp.exp(d - highest) for d in diffs]
        total = expon[0] + expon[1] + expon[2] + jnp.exp(-highest)
        codes = codes_ref[block]
        resid = [
            jnp.where(codes == float(a), 1.0, 0.0) - expon[a] / total for a in range(3)
        ]
        if block == 0:
            own = resid
        else:
            other = resid
    sums = [jnp.sum(x, axis=1, keepdims=True) for x in own]
    sums.append(-(sums[0] + sums[1] + sums[2]))
    line = jnp.zeros((LOCI, 128), f32)
    for a in range(Q):
        value = own_columns[a] + step_rate * (sums[a] / BATCH - field_decay * own_columns[a])
        line = line + jnp.where(lane == locus * Q + a, value, 0.0)
    new_fields_ref[...] = jnp.sum(line, axis=0, keepdims=True)
    for a in range(3):
        place = slice(a * LOCI, (a + 1) * LOCI)
        other_ref[place, :] = other[a]
        row_ref[place, :] = own[a]
        for s in range(DEPTH):
            z_ref[PLANES.index(s), place, :] = jnp.where(z_at >= s, own[a], other[a])


def fill(part, to_ref, at):
    pieces = [part[a * LOCI : (a + 1) * LOCI] for a in range(3)]
    pieces.append(-(pieces[0] + pieces[1] + pieces[2]))
    for a in range(Q):
        to_ref[pl.ds(at + a, LOCI, stride=Q), :] = pieces[a]


def masked(gradient, at):
    if at.start:
        return gradient
    col_at = lax.axis_index("col")
    spot = iota(gradient.shape, 0)
    same = (spot < PIECE) & ((col_at * PIECE + spot) // Q == iota(gradient.shape, 1) // Q)
    return jnp.where(same, 0.0, gradient)


def rows_kernel(band_ref, hot_cols_ref, *rest):
    row_refs, (out_ref, rows) = rest[:NEAR], rest[NEAR:]
    col_at = lax.axis_index("col")
    for step in range(COLS):
        fill(row_refs[step % NEAR][step // NEAR], rows, (col_at ^ step) * PIECE)
    rows_hi, rows_lo = split(rows[...].T)
    right = jnp.concatenate([rows_hi, rows_lo], axis=0)
    for at in CHUNKS:
        hot = hot_cols_ref[at, :]
        gradient = masked(mm(jnp.concatenate([hot, hot], axis=1), right), at)
        band = band_ref[at, :]
        out_ref[at, :] = band + step_rate * (gradient / BATCH - coupling_decay * band)


def cols_kernel(part_ref, z_ref, other_ref, core_ref, hot_rows_ref, out_ref, cols, new_ref, sems):
    row_at = lax.axis_index("row")
    z_at = lax.rem(row_at // 2, DEPTH)
    for j in range(TILES):
        if j % 2:
            part = core_ref[j // 2]
        elif j < HALF:
            part = z_ref[slot_of(z_at + j // 2)]
        else:
            part = other_ref[...]
        fill(part, cols, j * PIECE)
    hot_rows = hot_rows_ref[...]
    right = jnp.concatenate([hot_rows, hot_rows], axis=0)
    dead = row_at >= HALF
    copies = []
    for chunk, at in enumerate(CHUNKS):
        gradient = masked(mm(jnp.concatenate(split(cols[at, :]), axis=1), right), at)
        new = part_ref[at, :] + step_rate * (gradient / BATCH)
        if chunk == len(CHUNKS) - 1:
            spot = iota(new.shape, 0) + at.start
            new = jnp.where(dead & (spot >= HALF * PIECE), 0.0, new)
        new_ref[at, :] = new
        copies.append(pltpu.make_async_copy(new_ref.at[at], out_ref.at[at], sems.at[chunk]))
        copies[-1].start()
    for copy in copies:
        copy.wait()


COST = pl.CostEstimate(flops=4 * 10**10, bytes_accessed=10**6, transcendentals=0)


def call(kernel, outs, scratch=(), name=None, hbm=False, hbm_out=False, cost=None, loose=(), inputs=0):
    specs = {"in_specs": [pl.BlockSpec(memory_space=pltpu.HBM)] * 2} if hbm else {}
    if loose:
        specs["in_specs"] = [
            pl.BlockSpec(memory_space=pl.ANY if i in loose else pltpu.VMEM) for i in range(inputs)
        ]
    if hbm_out:
        specs["out_specs"] = pl.BlockSpec(memory_space=pltpu.HBM)
    return pl.pallas_call(
        kernel,
        out_shape=outs,
        scratch_shapes=list(scratch),
        compiler_params=pltpu.CompilerParams(
            vmem_limit_bytes=(52 if hbm else 24) * 1024 * 1024
        ),
        name=name,
        cost_estimate=cost,
        **specs,
    )


def arr(*shape, dtype=f32):
    return jax.ShapeDtypeStruct(shape, dtype)


def shards(seqs, fields, band):
    band_t = band.T
    piece = arr(SENT, BATCH)
    four = arr(NEAR, SENT, BATCH)
    eight = arr(DEPTH, SENT, BATCH)
    codes, mine, core, keep, give, hot, hot_rows = call(
        logits_kernel,
        (
            arr(2, LOCI, BATCH),
            eight,
            eight,
            four,
            four,
            arr(BATCH, 9 * 128, dtype=bf16),
            arr(SPAN, BATCH, dtype=bf16),
        ),
        [
            pltpu.VMEM((TILES, BATCH, 128), jnp.int32),
            pltpu.VMEM((BAND, SPAN), f32),
            pltpu.VMEM((SPAN, BATCH), f32),
            pltpu.VMEM((BAND, BATCH), f32),
            pltpu.SemaphoreType.DMA((TILES,)),
            pltpu.SemaphoreType.DMA((len(CHUNKS),)),
        ],
        "logit_parts",
        hbm=True,
    )(seqs, band_t)
    core = lax.ppermute(core, "row", SWAP_CORES)
    give = swap_cols(give, NEAR)
    z_send, last, *parts = call(
        combine_kernel, (eight, piece) + (piece,) * NEAR, name="combine"
    )(mine, core, keep, give)
    z_got = lax.all_to_all(z_send, "row", 0, 0, tiled=True, axis_index_groups=Z_GROUPS)
    row_got = [swap_cols(parts[step], step) for step in (3, 2, 1)] + [parts[0]]
    hot_cols, hot_rows = call(
        flip_kernel, (arr(BAND, BATCH, dtype=bf16), arr(BATCH, SPAN, dtype=bf16)), name="flip"
    )(hot, hot_rows)
    here = call(sum_kernel, arr(2 * SENT, BATCH), name="sum_parts", loose=(2, 3), inputs=8)(
        z_got, last, hot_cols, hot_rows, *row_got
    )
    there = lax.ppermute(here, "row", SWAP_HALVES)
    z_send, resid, other, new_fields = call(
        softmax_kernel,
        (eight, piece, piece, arr(1, 128)),
        name="softmax",
    )(here, there, codes, fields.reshape(-1, 128))
    across = swap_cols(resid, NEAR)
    z_all = lax.all_to_all(z_send, "row", 0, 0, tiled=True, axis_index_groups=Z_GROUPS)
    pair = call(pair_kernel, arr(2, SENT, BATCH), name="pair", cost=COST)(resid, across)
    row_all = [pair] + [swap_cols(pair, step) for step in range(1, NEAR)]
    core_all = lax.ppermute(
        call(choose_kernel, eight, name="choose")(z_all, other), "row", SWAP_CORES
    )
    part = call(
        rows_kernel, arr(BAND, SPAN), [pltpu.VMEM((SPAN, BATCH), f32)], "update_rows"
    )(band_t, hot_cols, *row_all)
    new_band_t = call(
        cols_kernel,
        arr(BAND, SPAN),
        [
            pltpu.VMEM((BAND, BATCH), f32),
            pltpu.VMEM((BAND, SPAN), f32),
            pltpu.SemaphoreType.DMA((len(CHUNKS),)),
        ],
        "update_cols",
        hbm_out=True,
    )(part, z_all, other, core_all, hot_rows)
    return new_band_t.T, new_fields[0, :PIECE]


def solution(mesh):
    in_specs = (P(), P(), P("row", "col"))
    out_specs = (P("row", "col"), P(("row", "col")))
    return jax.shard_map(shards, mesh=mesh, in_specs=in_specs, out_specs=out_specs, check_vma=False)
```

```python
import jax
import jax.numpy as jnp
from jax import lax
from jax.experimental import pallas as pl
from jax.experimental.pallas import tpu as pltpu
from jax.sharding import PartitionSpec as P

Q = 4
ROWS = 32
COLS = 8
HALF = 16
TILES = 17
PIECE = 64
LOCI = 16
SPAN = 512
BAND = TILES * PIECE
BATCH = 128
SENT = 3 * LOCI

step_rate = 1.0
coupling_decay = 0.25
field_decay = 0.1

DEPTH = 8
FIRST = [4, 5, 6, 7, 0, 1, 2, 3]
SECOND = [7, 6, 5, 4, 3, 2, 1, 0]


def z_exchange(x, planes):
    groups = [[(h * DEPTH + z) * 2 + k for z in planes] for h in range(2) for k in range(2)]
    return lax.all_to_all(x, "row", 0, 0, tiled=True, axis_index_groups=groups)


SWAP_CORES = [(i, i ^ 1) for i in range(ROWS)]
SWAP_HALVES = [(i, i ^ HALF) for i in range(ROWS)]


def swap_cols(x, step):
    return lax.ppermute(x, "col", [(i, i ^ step) for i in range(COLS)])


NEAR = 4
CHUNKS = [slice(0, 256), slice(256, 512), slice(512, 768), slice(768, BAND)]

f32 = jnp.float32
bf16 = jnp.bfloat16
NT = (((1,), (1,)), ((), ()))


def iota(shape, dim):
    return lax.broadcasted_iota(jnp.int32, shape, dim)


def split(x):
    hi = x.astype(bf16)
    return hi, (x - hi.astype(f32)).astype(bf16)


def mm(a, b):
    return jnp.dot(a, b, preferred_element_type=f32)


def logits_kernel(
    seqs_ref,
    band_ref,
    codes_ref,
    mine_ref,
    core_ref,
    keep_ref,
    give_ref,
    hot,
    hot_rows_ref,
    blocks,
    band,
    row_t,
    col_t,
    block_sems,
    band_sems,
):
    row_at = lax.axis_index("row")
    col_at = lax.axis_index("col")
    block_copies = []
    for j in range(TILES):
        start = pl.multiple_of(lax.rem(row_at + j, ROWS) * BATCH, BATCH)
        block_copies.append(
            pltpu.make_async_copy(
                seqs_ref.at[:, pl.ds(start, BATCH)], blocks.at[j], block_sems.at[j]
            )
        )
    band_copies = [
        pltpu.make_async_copy(band_ref.at[at], band.at[at], band_sems.at[i])
        for i, at in enumerate(CHUNKS)
    ]
    for copy in block_copies + band_copies:
        copy.start()
    lane = iota((BATCH, 128), 1)
    pick = (iota((128, 128), 0) == col_at * LOCI + lane % PIECE // Q).astype(f32).astype(bf16)
    pick_loci = (
        (iota((LOCI, 128), 1) == col_at * LOCI + iota((LOCI, 128), 0)).astype(f32).astype(bf16)
    )
    spread = (iota((SPAN, 128), 1) == iota((SPAN, 128), 0) // Q).astype(f32).astype(bf16)
    state = (lane % Q).astype(f32)
    dead = row_at >= HALF

    for copy in block_copies:
        copy.wait()

    def block(j):
        return blocks[j].astype(f32).astype(bf16)

    own = block(0)
    codes_ref[0] = lax.dot_general(pick_loci, own, NT, preferred_element_type=f32)
    codes_rows = lax.dot_general(spread, own, NT, preferred_element_type=f32)
    hot_rows = (codes_rows == (iota((SPAN, 128), 0) % Q).astype(f32)).astype(f32).astype(bf16)
    hot_rows_ref[...] = hot_rows
    for pair in range(9):
        left = block(2 * pair) if pair else own
        codes = mm(left, pick)
        if pair < 8:
            codes = jnp.where(lane < PIECE, codes, mm(block(2 * pair + 1), pick))
        else:
            codes_ref[1] = lax.dot_general(pick_loci, left, NT, preferred_element_type=f32)
            codes = jnp.where((lane < PIECE) & jnp.logical_not(dead), codes, -1.0)
        hot[:, pair * 128 : pair * 128 + 128] = (codes == state).astype(f32).astype(bf16)
    part = None
    for chunk, at in enumerate(CHUNKS):
        if chunk % 2 == 0:
            band_copies[chunk].wait()
            band_copies[chunk + 1].wait()
        hi, lo = split(band[at, :])
        col_t[at, :] = mm(hi, hot_rows) + mm(lo, hot_rows)
        term = mm(hot[:, at], hi) + mm(hot[:, at], lo)
        part = term if part is None else part + term
    row_t[...] = part.T
    last = col_t[pl.ds(3, TILES * LOCI, stride=Q), :]
    for a in range(3):
        diff = col_t[pl.ds(a, TILES * LOCI, stride=Q), :] - last
        place = slice(a * LOCI, (a + 1) * LOCI)
        for e in range(DEPTH):
            core_ref[e, place, :] = diff[(2 * e + 1) * LOCI : (2 * e + 2) * LOCI]
            value = diff[(2 * e + 2) * LOCI : (2 * e + 3) * LOCI]
            if e == DEPTH - 1:
                value = jnp.where(dead, 0.0, value)
            mine_ref[e, place, :] = value
    for step in range(COLS):
        start = (col_at ^ step) * PIECE
        to = keep_ref if step < NEAR else give_ref
        last = row_t[pl.ds(start + 3, LOCI, stride=Q), :]
        for a in range(3):
            place = slice(a * LOCI, (a + 1) * LOCI)
            to[step % NEAR, place, :] = row_t[pl.ds(start + a, LOCI, stride=Q), :] - last


def first_slot(z):
    return lax.rem(z + 4, DEPTH)


def second_slot(z):
    return 7 - lax.rem(z, DEPTH)


def place_of():
    row_at = lax.axis_index("row")
    return row_at, lax.rem(row_at, 2) == 1, lax.rem(row_at // 2, DEPTH)


def combine_kernel(mine_ref, core_ref, keep_ref, got_ref, z_ref, last_ref, *part_refs):
    _, odd, z_at = place_of()
    for d in range(DEPTH + 1):
        lower = core_ref[d] if d < DEPTH else jnp.zeros((SENT, BATCH), f32)
        upper = core_ref[d - 1] if d else jnp.zeros((SENT, BATCH), f32)
        value = jnp.where(odd, lower, upper)
        if d:
            value = value + mine_ref[d - 1]
        if d < DEPTH:
            z_ref[first_slot(z_at + d)] = value
        else:
            last_ref[...] = value
    for step in range(NEAR):
        part_refs[step][...] = keep_ref[step] + got_ref[step]


def sum_kernel(z_ref, last_ref, hot_ref, hot_rows_ref, *rest):
    del hot_ref, hot_rows_ref
    row_refs, out_ref = rest[:NEAR], rest[NEAR]
    _, _, z_at = place_of()
    own = row_refs[0][...]
    for step in range(1, NEAR):
        own = own + row_refs[step][...]
    other = last_ref[...]
    for s in range(DEPTH):
        part = z_ref[FIRST.index(s)]
        own = own + jnp.where(s <= z_at, part, 0.0)
        other = other + jnp.where(s > z_at, part, 0.0)
    out_ref[:SENT, :] = own
    out_ref[SENT:, :] = other


def choose_kernel(z_ref, other_ref, core_ref):
    _, odd, z_at = place_of()
    for e in range(DEPTH):
        lower = z_ref[second_slot(z_at + e)]
        upper = z_ref[second_slot(z_at + e + 1)] if e < DEPTH - 1 else other_ref[...]
        core_ref[e] = jnp.where(odd, lower, upper)


def flip_kernel(hot_ref, hot_rows_ref, hot_t_ref, hot_rows_t_ref):
    eye = (iota((128, 128), 0) == iota((128, 128), 1)).astype(f32).astype(bf16)
    for j in range(9):
        at = slice(j * 128, min(BAND, (j + 1) * 128))
        turned = lax.dot_general(
            hot_ref[:, at], eye, (((0,), (0,)), ((), ())), preferred_element_type=f32
        )
        hot_t_ref[at, :] = turned.astype(bf16)
    turned = lax.dot_general(eye, hot_rows_ref[...], NT, preferred_element_type=f32)
    hot_rows_t_ref[...] = turned.astype(bf16)


def pair_kernel(own_ref, got_ref, out_ref):
    out_ref[0] = own_ref[...]
    out_ref[1] = got_ref[...]


def softmax_kernel(
    here_ref, there_ref, codes_ref, fields_ref, z_ref, row_ref, other_ref, new_fields_ref
):
    row_at = lax.axis_index("row")
    col_at = lax.axis_index("col")
    z_at = lax.rem(row_at // 2, DEPTH)
    lane = iota((LOCI, 128), 1)
    locus = iota((LOCI, 128), 0)
    start = col_at % 2 * PIECE
    own = []
    other = []
    columns = []
    for block in range(2):
        block_at = lax.rem(row_at + block * HALF, ROWS)
        line = fields_ref[pl.ds(block_at * 4 + col_at // 2, 1), :]
        columns = [
            jnp.sum(jnp.where(lane == start + locus * Q + a, line, 0.0), axis=1, keepdims=True)
            for a in range(Q)
        ]
        if block == 0:
            own_columns = columns
        diffs = []
        for a in range(3):
            here = here_ref[block * SENT + a * LOCI : block * SENT + (a + 1) * LOCI, :]
            flip = (1 - block) * SENT + a * LOCI
            there = there_ref[flip : flip + LOCI, :]
            diffs.append(here + there + (columns[a] - columns[3]))
        highest = jnp.maximum(jnp.maximum(diffs[0], diffs[1]), jnp.maximum(diffs[2], 0.0))
        expon = [jnp.exp(d - highest) for d in diffs]
        total = expon[0] + expon[1] + expon[2] + jnp.exp(-highest)
        codes = codes_ref[block]
        resid = [
            jnp.where(codes == float(a), 1.0, 0.0) - expon[a] / total for a in range(3)
        ]
        if block == 0:
            own = resid
        else:
            other = resid
    sums = [jnp.sum(x, axis=1, keepdims=True) for x in own]
    sums.append(-(sums[0] + sums[1] + sums[2]))
    line = jnp.zeros((LOCI, 128), f32)
    for a in range(Q):
        value = own_columns[a] + step_rate * (sums[a] / BATCH - field_decay * own_columns[a])
        line = line + jnp.where(lane == locus * Q + a, value, 0.0)
    new_fields_ref[...] = jnp.sum(line, axis=0, keepdims=True)
    for a in range(3):
        place = slice(a * LOCI, (a + 1) * LOCI)
        other_ref[place, :] = other[a]
        row_ref[place, :] = own[a]
        for s in range(DEPTH):
            z_ref[SECOND.index(s), place, :] = jnp.where(z_at >= s, own[a], other[a])


def fill(part, to_ref, at):
    pieces = [part[a * LOCI : (a + 1) * LOCI] for a in range(3)]
    pieces.append(-(pieces[0] + pieces[1] + pieces[2]))
    for a in range(Q):
        to_ref[pl.ds(at + a, LOCI, stride=Q), :] = pieces[a]


def masked(gradient, at):
    if at.start:
        return gradient
    col_at = lax.axis_index("col")
    spot = iota(gradient.shape, 0)
    same = (spot < PIECE) & ((col_at * PIECE + spot) // Q == iota(gradient.shape, 1) // Q)
    return jnp.where(same, 0.0, gradient)


def rows_kernel(band_ref, hot_cols_ref, *rest):
    row_refs, (out_ref, rows) = rest[:NEAR], rest[NEAR:]
    col_at = lax.axis_index("col")
    for step in range(COLS):
        fill(row_refs[step % NEAR][step // NEAR], rows, (col_at ^ step) * PIECE)
    rows_hi, rows_lo = split(rows[...].T)
    right = jnp.concatenate([rows_hi, rows_lo], axis=0)
    for at in CHUNKS:
        hot = hot_cols_ref[at, :]
        gradient = masked(mm(jnp.concatenate([hot, hot], axis=1), right), at)
        band = band_ref[at, :]
        out_ref[at, :] = band + step_rate * (gradient / BATCH - coupling_decay * band)


def cols_kernel(part_ref, z_ref, other_ref, core_ref, hot_rows_ref, out_ref, cols, new_ref, sems):
    row_at = lax.axis_index("row")
    z_at = lax.rem(row_at // 2, DEPTH)
    for j in range(TILES):
        if j % 2:
            part = core_ref[j // 2]
        elif j < HALF:
            part = z_ref[second_slot(z_at + j // 2)]
        else:
            part = other_ref[...]
        fill(part, cols, j * PIECE)
    hot_rows = hot_rows_ref[...]
    right = jnp.concatenate([hot_rows, hot_rows], axis=0)
    dead = row_at >= HALF
    copies = []
    for chunk, at in enumerate(CHUNKS):
        gradient = masked(mm(jnp.concatenate(split(cols[at, :]), axis=1), right), at)
        new = part_ref[at, :] + step_rate * (gradient / BATCH)
        if chunk == len(CHUNKS) - 1:
            spot = iota(new.shape, 0) + at.start
            new = jnp.where(dead & (spot >= HALF * PIECE), 0.0, new)
        new_ref[at, :] = new
        copies.append(pltpu.make_async_copy(new_ref.at[at], out_ref.at[at], sems.at[chunk]))
        copies[-1].start()
    for copy in copies:
        copy.wait()


COST = pl.CostEstimate(flops=4 * 10**10, bytes_accessed=10**6, transcendentals=0)


def call(kernel, outs, scratch=(), name=None, hbm=False, hbm_out=False, cost=None, loose=(), inputs=0):
    specs = {"in_specs": [pl.BlockSpec(memory_space=pltpu.HBM)] * 2} if hbm else {}
    if loose:
        specs["in_specs"] = [
            pl.BlockSpec(memory_space=pl.ANY if i in loose else pltpu.VMEM) for i in range(inputs)
        ]
    if hbm_out:
        specs["out_specs"] = pl.BlockSpec(memory_space=pltpu.HBM)
    return pl.pallas_call(
        kernel,
        out_shape=outs,
        scratch_shapes=list(scratch),
        compiler_params=pltpu.CompilerParams(
            vmem_limit_bytes=(52 if hbm else 24) * 1024 * 1024
        ),
        name=name,
        cost_estimate=cost,
        **specs,
    )


def arr(*shape, dtype=f32):
    return jax.ShapeDtypeStruct(shape, dtype)


def shards(seqs, fields, band):
    band_t = band.T
    piece = arr(SENT, BATCH)
    four = arr(NEAR, SENT, BATCH)
    eight = arr(DEPTH, SENT, BATCH)
    codes, mine, core, keep, give, hot, hot_rows = call(
        logits_kernel,
        (
            arr(2, LOCI, BATCH),
            eight,
            eight,
            four,
            four,
            arr(BATCH, 9 * 128, dtype=bf16),
            arr(SPAN, BATCH, dtype=bf16),
        ),
        [
            pltpu.VMEM((TILES, BATCH, 128), jnp.int32),
            pltpu.VMEM((BAND, SPAN), f32),
            pltpu.VMEM((SPAN, BATCH), f32),
            pltpu.VMEM((BAND, BATCH), f32),
            pltpu.SemaphoreType.DMA((TILES,)),
            pltpu.SemaphoreType.DMA((len(CHUNKS),)),
        ],
        "logit_parts",
        hbm=True,
    )(seqs, band_t)
    core = lax.ppermute(core, "row", SWAP_CORES)
    give = swap_cols(give, NEAR)
    z_send, last, *parts = call(
        combine_kernel, (eight, piece) + (piece,) * NEAR, name="combine"
    )(mine, core, keep, give)
    z_got = z_exchange(z_send, FIRST)
    row_got = [swap_cols(parts[step], step) for step in (3, 2, 1)] + [parts[0]]
    hot_cols, hot_rows = call(
        flip_kernel, (arr(BAND, BATCH, dtype=bf16), arr(BATCH, SPAN, dtype=bf16)), name="flip"
    )(hot, hot_rows)
    here = call(sum_kernel, arr(2 * SENT, BATCH), name="sum_parts", loose=(2, 3), inputs=8)(
        z_got, last, hot_cols, hot_rows, *row_got
    )
    there = lax.ppermute(here, "row", SWAP_HALVES)
    z_send, resid, other, new_fields = call(
        softmax_kernel,
        (eight, piece, piece, arr(1, 128)),
        name="softmax",
    )(here, there, codes, fields.reshape(-1, 128))
    across = swap_cols(resid, NEAR)
    z_all = z_exchange(z_send, SECOND)
    pair = call(pair_kernel, arr(2, SENT, BATCH), name="pair", cost=COST)(resid, across)
    row_all = [pair] + [swap_cols(pair, step) for step in range(1, NEAR)]
    core_all = lax.ppermute(
        call(choose_kernel, eight, name="choose")(z_all, other), "row", SWAP_CORES
    )
    part = call(
        rows_kernel, arr(BAND, SPAN), [pltpu.VMEM((SPAN, BATCH), f32)], "update_rows"
    )(band_t, hot_cols, *row_all)
    new_band_t = call(
        cols_kernel,
        arr(BAND, SPAN),
        [
            pltpu.VMEM((BAND, BATCH), f32),
            pltpu.VMEM((BAND, SPAN), f32),
            pltpu.SemaphoreType.DMA((len(CHUNKS),)),
        ],
        "update_cols",
        hbm_out=True,
    )(part, z_all, other, core_all, hot_rows)
    return new_band_t.T, new_fields[0, :PIECE]


def solution(mesh):
    in_specs = (P(), P(), P("row", "col"))
    out_specs = (P("row", "col"), P(("row", "col")))
    return jax.shard_map(shards, mesh=mesh, in_specs=in_specs, out_specs=out_specs, check_vma=False)
```

```python
import jax
import jax.numpy as jnp
from jax import lax
from jax.experimental import pallas as pl
from jax.experimental.pallas import tpu as pltpu
from jax.sharding import PartitionSpec as P

Q = 4
ROWS = 32
COLS = 8
HALF = 16
TILES = 17
PIECE = 64
LOCI = 16
SPAN = 512
BAND = TILES * PIECE
BATCH = 128
SENT = 3 * LOCI

step_rate = 1.0
coupling_decay = 0.25
field_decay = 0.1

DEPTH = 8
FIRST = [4, 5, 6, 7, 0, 1, 2, 3]
SECOND = [7, 6, 5, 4, 3, 2, 1, 0]


def z_exchange(x, planes):
    groups = [[(h * DEPTH + z) * 2 + k for z in planes] for h in range(2) for k in range(2)]
    return lax.all_to_all(x, "row", 0, 0, tiled=True, axis_index_groups=groups)


SWAP_CORES = [(i, i ^ 1) for i in range(ROWS)]
SWAP_HALVES = [(i, i ^ HALF) for i in range(ROWS)]


def swap_cols(x, step):
    return lax.ppermute(x, "col", [(i, i ^ step) for i in range(COLS)])


NEAR = 4
CHUNKS = [slice(0, 256), slice(256, 512), slice(512, 768), slice(768, BAND)]

f32 = jnp.float32
bf16 = jnp.bfloat16
NT = (((1,), (1,)), ((), ()))


def iota(shape, dim):
    return lax.broadcasted_iota(jnp.int32, shape, dim)


def split(x):
    hi = x.astype(bf16)
    return hi, (x - hi.astype(f32)).astype(bf16)


def mm(a, b):
    return jnp.dot(a, b, preferred_element_type=f32)


def logits_kernel(
    seqs_ref,
    band_ref,
    codes_ref,
    mine_ref,
    core_ref,
    keep_ref,
    give_ref,
    hot,
    hot_rows_ref,
    blocks,
    band,
    row_t,
    col_t,
    block_sems,
    band_sems,
):
    row_at = lax.axis_index("row")
    col_at = lax.axis_index("col")
    block_copies = []
    for j in range(TILES):
        start = pl.multiple_of(lax.rem(row_at + j, ROWS) * BATCH, BATCH)
        block_copies.append(
            pltpu.make_async_copy(
                seqs_ref.at[:, pl.ds(start, BATCH)], blocks.at[j], block_sems.at[j]
            )
        )
    band_copies = [
        pltpu.make_async_copy(band_ref.at[at], band.at[at], band_sems.at[i])
        for i, at in enumerate(CHUNKS)
    ]
    for copy in block_copies + band_copies:
        copy.start()
    lane = iota((BATCH, 128), 1)
    pick = (iota((128, 128), 0) == col_at * LOCI + lane % PIECE // Q).astype(f32).astype(bf16)
    pick_loci = (
        (iota((LOCI, 128), 1) == col_at * LOCI + iota((LOCI, 128), 0)).astype(f32).astype(bf16)
    )
    spread = (iota((SPAN, 128), 1) == iota((SPAN, 128), 0) // Q).astype(f32).astype(bf16)
    state = (lane % Q).astype(f32)
    dead = row_at >= HALF

    for copy in block_copies:
        copy.wait()

    def block(j):
        return blocks[j].astype(f32).astype(bf16)

    own = block(0)
    codes_ref[0] = lax.dot_general(pick_loci, own, NT, preferred_element_type=f32)
    codes_rows = lax.dot_general(spread, own, NT, preferred_element_type=f32)
    hot_rows = (codes_rows == (iota((SPAN, 128), 0) % Q).astype(f32)).astype(f32).astype(bf16)
    hot_rows_ref[...] = hot_rows
    for pair in range(9):
        left = block(2 * pair) if pair else own
        codes = mm(left, pick)
        if pair < 8:
            codes = jnp.where(lane < PIECE, codes, mm(block(2 * pair + 1), pick))
        else:
            codes_ref[1] = lax.dot_general(pick_loci, left, NT, preferred_element_type=f32)
            codes = jnp.where((lane < PIECE) & jnp.logical_not(dead), codes, -1.0)
        hot[:, pair * 128 : pair * 128 + 128] = (codes == state).astype(f32).astype(bf16)
    part = None
    for chunk, at in enumerate(CHUNKS):
        if chunk % 2 == 0:
            band_copies[chunk].wait()
            band_copies[chunk + 1].wait()
        hi, lo = split(band[at, :])
        col_t[at, :] = mm(hi, hot_rows) + mm(lo, hot_rows)
        term = mm(hot[:, at], hi) + mm(hot[:, at], lo)
        part = term if part is None else part + term
    row_t[...] = part.T
    last = col_t[pl.ds(3, TILES * LOCI, stride=Q), :]
    for a in range(3):
        diff = col_t[pl.ds(a, TILES * LOCI, stride=Q), :] - last
        place = slice(a * LOCI, (a + 1) * LOCI)
        for e in range(DEPTH):
            core_ref[e, place, :] = diff[(2 * e + 1) * LOCI : (2 * e + 2) * LOCI]
            value = diff[(2 * e + 2) * LOCI : (2 * e + 3) * LOCI]
            if e == DEPTH - 1:
                value = jnp.where(dead, 0.0, value)
            mine_ref[e, place, :] = value
    for step in range(COLS):
        start = (col_at ^ step) * PIECE
        to = keep_ref if step < NEAR else give_ref
        last = row_t[pl.ds(start + 3, LOCI, stride=Q), :]
        for a in range(3):
            place = slice(a * LOCI, (a + 1) * LOCI)
            to[step % NEAR, place, :] = row_t[pl.ds(start + a, LOCI, stride=Q), :] - last


def first_slot(z):
    return lax.rem(z + 4, DEPTH)


def second_slot(z):
    return 7 - lax.rem(z, DEPTH)


def place_of():
    row_at = lax.axis_index("row")
    return row_at, lax.rem(row_at, 2) == 1, lax.rem(row_at // 2, DEPTH)


def combine_kernel(mine_ref, core_ref, z_ref, last_ref):
    _, odd, z_at = place_of()
    for d in range(DEPTH + 1):
        lower = core_ref[d] if d < DEPTH else jnp.zeros((SENT, BATCH), f32)
        upper = core_ref[d - 1] if d else jnp.zeros((SENT, BATCH), f32)
        value = jnp.where(odd, lower, upper)
        if d:
            value = value + mine_ref[d - 1]
        if d < DEPTH:
            z_ref[first_slot(z_at + d)] = value
        else:
            last_ref[...] = value


def add_kernel(keep_ref, got_ref, last_ref, *part_refs):
    del last_ref
    for step in range(NEAR):
        part_refs[step][...] = keep_ref[step] + got_ref[step]


def sum_kernel(z_ref, last_ref, hot_ref, hot_rows_ref, *rest):
    del hot_ref, hot_rows_ref
    row_refs, out_ref = rest[:NEAR], rest[NEAR]
    _, _, z_at = place_of()
    own = row_refs[0][...]
    for step in range(1, NEAR):
        own = own + row_refs[step][...]
    other = last_ref[...]
    for s in range(DEPTH):
        part = z_ref[FIRST.index(s)]
        own = own + jnp.where(s <= z_at, part, 0.0)
        other = other + jnp.where(s > z_at, part, 0.0)
    out_ref[:SENT, :] = own
    out_ref[SENT:, :] = other


def choose_kernel(z_ref, other_ref, core_ref):
    _, odd, z_at = place_of()
    for e in range(DEPTH):
        lower = z_ref[second_slot(z_at + e)]
        upper = z_ref[second_slot(z_at + e + 1)] if e < DEPTH - 1 else other_ref[...]
        core_ref[e] = jnp.where(odd, lower, upper)


def flip_kernel(hot_ref, hot_rows_ref, hot_t_ref, hot_rows_t_ref):
    eye = (iota((128, 128), 0) == iota((128, 128), 1)).astype(f32).astype(bf16)
    for j in range(9):
        at = slice(j * 128, min(BAND, (j + 1) * 128))
        turned = lax.dot_general(
            hot_ref[:, at], eye, (((0,), (0,)), ((), ())), preferred_element_type=f32
        )
        hot_t_ref[at, :] = turned.astype(bf16)
    turned = lax.dot_general(eye, hot_rows_ref[...], NT, preferred_element_type=f32)
    hot_rows_t_ref[...] = turned.astype(bf16)


def pair_kernel(own_ref, got_ref, out_ref):
    out_ref[0] = own_ref[...]
    out_ref[1] = got_ref[...]


def softmax_kernel(
    here_ref, there_ref, codes_ref, fields_ref, z_ref, row_ref, other_ref, new_fields_ref
):
    row_at = lax.axis_index("row")
    col_at = lax.axis_index("col")
    z_at = lax.rem(row_at // 2, DEPTH)
    lane = iota((LOCI, 128), 1)
    locus = iota((LOCI, 128), 0)
    start = col_at % 2 * PIECE
    own = []
    other = []
    columns = []
    for block in range(2):
        block_at = lax.rem(row_at + block * HALF, ROWS)
        line = fields_ref[pl.ds(block_at * 4 + col_at // 2, 1), :]
        columns = [
            jnp.sum(jnp.where(lane == start + locus * Q + a, line, 0.0), axis=1, keepdims=True)
            for a in range(Q)
        ]
        if block == 0:
            own_columns = columns
        diffs = []
        for a in range(3):
            here = here_ref[block * SENT + a * LOCI : block * SENT + (a + 1) * LOCI, :]
            flip = (1 - block) * SENT + a * LOCI
            there = there_ref[flip : flip + LOCI, :]
            diffs.append(here + there + (columns[a] - columns[3]))
        highest = jnp.maximum(jnp.maximum(diffs[0], diffs[1]), jnp.maximum(diffs[2], 0.0))
        expon = [jnp.exp(d - highest) for d in diffs]
        total = expon[0] + expon[1] + expon[2] + jnp.exp(-highest)
        codes = codes_ref[block]
        resid = [
            jnp.where(codes == float(a), 1.0, 0.0) - expon[a] / total for a in range(3)
        ]
        if block == 0:
            own = resid
        else:
            other = resid
    sums = [jnp.sum(x, axis=1, keepdims=True) for x in own]
    sums.append(-(sums[0] + sums[1] + sums[2]))
    line = jnp.zeros((LOCI, 128), f32)
    for a in range(Q):
        value = own_columns[a] + step_rate * (sums[a] / BATCH - field_decay * own_columns[a])
        line = line + jnp.where(lane == locus * Q + a, value, 0.0)
    new_fields_ref[...] = jnp.sum(line, axis=0, keepdims=True)
    for a in range(3):
        place = slice(a * LOCI, (a + 1) * LOCI)
        other_ref[place, :] = other[a]
        row_ref[place, :] = own[a]
        for s in range(DEPTH):
            z_ref[SECOND.index(s), place, :] = jnp.where(z_at >= s, own[a], other[a])


def fill(part, to_ref, at):
    pieces = [part[a * LOCI : (a + 1) * LOCI] for a in range(3)]
    pieces.append(-(pieces[0] + pieces[1] + pieces[2]))
    for a in range(Q):
        to_ref[pl.ds(at + a, LOCI, stride=Q), :] = pieces[a]


def masked(gradient, at):
    if at.start:
        return gradient
    col_at = lax.axis_index("col")
    spot = iota(gradient.shape, 0)
    same = (spot < PIECE) & ((col_at * PIECE + spot) // Q == iota(gradient.shape, 1) // Q)
    return jnp.where(same, 0.0, gradient)


def rows_kernel(band_ref, hot_cols_ref, *rest):
    row_refs, (out_ref, rows) = rest[:NEAR], rest[NEAR:]
    col_at = lax.axis_index("col")
    for step in range(COLS):
        fill(row_refs[step % NEAR][step // NEAR], rows, (col_at ^ step) * PIECE)
    rows_hi, rows_lo = split(rows[...].T)
    right = jnp.concatenate([rows_hi, rows_lo], axis=0)
    for at in CHUNKS:
        hot = hot_cols_ref[at, :]
        gradient = masked(mm(jnp.concatenate([hot, hot], axis=1), right), at)
        band = band_ref[at, :]
        out_ref[at, :] = band + step_rate * (gradient / BATCH - coupling_decay * band)


def cols_kernel(part_ref, z_ref, other_ref, core_ref, hot_rows_ref, out_ref, cols, new_ref, sems):
    row_at = lax.axis_index("row")
    z_at = lax.rem(row_at // 2, DEPTH)
    for j in range(TILES):
        if j % 2:
            part = core_ref[j // 2]
        elif j < HALF:
            part = z_ref[second_slot(z_at + j // 2)]
        else:
            part = other_ref[...]
        fill(part, cols, j * PIECE)
    hot_rows = hot_rows_ref[...]
    right = jnp.concatenate([hot_rows, hot_rows], axis=0)
    dead = row_at >= HALF
    copies = []
    for chunk, at in enumerate(CHUNKS):
        gradient = masked(mm(jnp.concatenate(split(cols[at, :]), axis=1), right), at)
        new = part_ref[at, :] + step_rate * (gradient / BATCH)
        if chunk == len(CHUNKS) - 1:
            spot = iota(new.shape, 0) + at.start
            new = jnp.where(dead & (spot >= HALF * PIECE), 0.0, new)
        new_ref[at, :] = new
        copies.append(pltpu.make_async_copy(new_ref.at[at], out_ref.at[at], sems.at[chunk]))
        copies[-1].start()
    for copy in copies:
        copy.wait()


COST = pl.CostEstimate(flops=4 * 10**10, bytes_accessed=10**6, transcendentals=0)


def call(kernel, outs, scratch=(), name=None, hbm=False, hbm_out=False, cost=None, loose=(), inputs=0):
    specs = {"in_specs": [pl.BlockSpec(memory_space=pltpu.HBM)] * 2} if hbm else {}
    if loose:
        specs["in_specs"] = [
            pl.BlockSpec(memory_space=pl.ANY if i in loose else pltpu.VMEM) for i in range(inputs)
        ]
    if hbm_out:
        specs["out_specs"] = pl.BlockSpec(memory_space=pltpu.HBM)
    return pl.pallas_call(
        kernel,
        out_shape=outs,
        scratch_shapes=list(scratch),
        compiler_params=pltpu.CompilerParams(
            vmem_limit_bytes=(52 if hbm else 24) * 1024 * 1024
        ),
        name=name,
        cost_estimate=cost,
        **specs,
    )


def arr(*shape, dtype=f32):
    return jax.ShapeDtypeStruct(shape, dtype)


def shards(seqs, fields, band):
    band_t = band.T
    piece = arr(SENT, BATCH)
    four = arr(NEAR, SENT, BATCH)
    eight = arr(DEPTH, SENT, BATCH)
    codes, mine, core, keep, give, hot, hot_rows = call(
        logits_kernel,
        (
            arr(2, LOCI, BATCH),
            eight,
            eight,
            four,
            four,
            arr(BATCH, 9 * 128, dtype=bf16),
            arr(SPAN, BATCH, dtype=bf16),
        ),
        [
            pltpu.VMEM((TILES, BATCH, 128), jnp.int32),
            pltpu.VMEM((BAND, SPAN), f32),
            pltpu.VMEM((SPAN, BATCH), f32),
            pltpu.VMEM((BAND, BATCH), f32),
            pltpu.SemaphoreType.DMA((TILES,)),
            pltpu.SemaphoreType.DMA((len(CHUNKS),)),
        ],
        "logit_parts",
        hbm=True,
    )(seqs, band_t)
    core = lax.ppermute(core, "row", SWAP_CORES)
    give = swap_cols(give, NEAR)
    z_send, last = call(combine_kernel, (eight, piece), name="combine")(mine, core)
    parts = call(add_kernel, (piece,) * NEAR, name="add_halves", cost=COST, loose=(2,), inputs=3)(
        keep, give, last
    )
    z_got = z_exchange(z_send, FIRST)
    row_got = [swap_cols(parts[step], step) for step in (3, 2, 1)] + [parts[0]]
    hot_cols, hot_rows = call(
        flip_kernel, (arr(BAND, BATCH, dtype=bf16), arr(BATCH, SPAN, dtype=bf16)), name="flip"
    )(hot, hot_rows)
    here = call(sum_kernel, arr(2 * SENT, BATCH), name="sum_parts", loose=(2, 3), inputs=8)(
        z_got, last, hot_cols, hot_rows, *row_got
    )
    there = lax.ppermute(here, "row", SWAP_HALVES)
    z_send, resid, other, new_fields = call(
        softmax_kernel,
        (eight, piece, piece, arr(1, 128)),
        name="softmax",
    )(here, there, codes, fields.reshape(-1, 128))
    across = swap_cols(resid, NEAR)
    z_all = z_exchange(z_send, SECOND)
    pair = call(pair_kernel, arr(2, SENT, BATCH), name="pair", cost=COST)(resid, across)
    row_all = [pair] + [swap_cols(pair, step) for step in range(1, NEAR)]
    core_all = lax.ppermute(
        call(choose_kernel, eight, name="choose")(z_all, other), "row", SWAP_CORES
    )
    part = call(
        rows_kernel, arr(BAND, SPAN), [pltpu.VMEM((SPAN, BATCH), f32)], "update_rows"
    )(band_t, hot_cols, *row_all)
    new_band_t = call(
        cols_kernel,
        arr(BAND, SPAN),
        [
            pltpu.VMEM((BAND, BATCH), f32),
            pltpu.VMEM((BAND, SPAN), f32),
            pltpu.SemaphoreType.DMA((len(CHUNKS),)),
        ],
        "update_cols",
        hbm_out=True,
    )(part, z_all, other, core_all, hot_rows)
    return new_band_t.T, new_fields[0, :PIECE]


def solution(mesh):
    in_specs = (P(), P(), P("row", "col"))
    out_specs = (P("row", "col"), P(("row", "col")))
    return jax.shard_map(shards, mesh=mesh, in_specs=in_specs, out_specs=out_specs, check_vma=False)
```

```python
import jax
import jax.numpy as jnp
from jax import lax
from jax.experimental import pallas as pl
from jax.experimental.pallas import tpu as pltpu
from jax.sharding import PartitionSpec as P

Q = 4
ROWS = 32
COLS = 8
HALF = 16
TILES = 17
PIECE = 64
LOCI = 16
SPAN = 512
BAND = TILES * PIECE
BATCH = 128
SENT = 3 * LOCI

step_rate = 1.0
coupling_decay = 0.25
field_decay = 0.1

DEPTH = 8
FIRST = [4, 5, 6, 7, 0, 1, 2, 3]
SECOND = [7, 6, 5, 4, 3, 2, 1, 0]


def z_exchange(x, planes):
    groups = [[(h * DEPTH + z) * 2 + k for z in planes] for h in range(2) for k in range(2)]
    return lax.all_to_all(x, "row", 0, 0, tiled=True, axis_index_groups=groups)


SWAP_CORES = [(i, i ^ 1) for i in range(ROWS)]
SWAP_HALVES = [(i, i ^ HALF) for i in range(ROWS)]


def swap_cols(x, step):
    return lax.ppermute(x, "col", [(i, i ^ step) for i in range(COLS)])


NEAR = 4
CHUNKS = [slice(0, 256), slice(256, 512), slice(512, 768), slice(768, BAND)]

f32 = jnp.float32
bf16 = jnp.bfloat16
NT = (((1,), (1,)), ((), ()))


def iota(shape, dim):
    return lax.broadcasted_iota(jnp.int32, shape, dim)


def split(x):
    hi = x.astype(bf16)
    return hi, (x - hi.astype(f32)).astype(bf16)


def mm(a, b):
    return jnp.dot(a, b, preferred_element_type=f32)


def logits_kernel(
    seqs_ref,
    band_ref,
    codes_ref,
    mine_ref,
    core_ref,
    keep_ref,
    give_ref,
    hot,
    hot_rows_ref,
    blocks,
    band,
    row_t,
    col_t,
    block_sems,
    band_sems,
):
    row_at = lax.axis_index("row")
    col_at = lax.axis_index("col")
    block_copies = []
    for j in range(TILES):
        start = pl.multiple_of(lax.rem(row_at + j, ROWS) * BATCH, BATCH)
        block_copies.append(
            pltpu.make_async_copy(
                seqs_ref.at[:, pl.ds(start, BATCH)], blocks.at[j], block_sems.at[j]
            )
        )
    band_copies = [
        pltpu.make_async_copy(band_ref.at[at], band.at[at], band_sems.at[i])
        for i, at in enumerate(CHUNKS)
    ]
    for copy in block_copies + band_copies:
        copy.start()
    lane = iota((BATCH, 128), 1)
    pick = (iota((128, 128), 0) == col_at * LOCI + lane % PIECE // Q).astype(f32).astype(bf16)
    pick_loci = (
        (iota((LOCI, 128), 1) == col_at * LOCI + iota((LOCI, 128), 0)).astype(f32).astype(bf16)
    )
    spread = (iota((SPAN, 128), 1) == iota((SPAN, 128), 0) // Q).astype(f32).astype(bf16)
    state = (lane % Q).astype(f32)
    dead = row_at >= HALF

    for copy in block_copies:
        copy.wait()

    def block(j):
        return blocks[j].astype(f32).astype(bf16)

    own = block(0)
    codes_ref[0] = lax.dot_general(pick_loci, own, NT, preferred_element_type=f32)
    codes_rows = lax.dot_general(spread, own, NT, preferred_element_type=f32)
    hot_rows = (codes_rows == (iota((SPAN, 128), 0) % Q).astype(f32)).astype(f32).astype(bf16)
    hot_rows_ref[...] = hot_rows
    for pair in range(9):
        left = block(2 * pair) if pair else own
        codes = mm(left, pick)
        if pair < 8:
            codes = jnp.where(lane < PIECE, codes, mm(block(2 * pair + 1), pick))
        else:
            codes_ref[1] = lax.dot_general(pick_loci, left, NT, preferred_element_type=f32)
            codes = jnp.where((lane < PIECE) & jnp.logical_not(dead), codes, -1.0)
        hot[:, pair * 128 : pair * 128 + 128] = (codes == state).astype(f32).astype(bf16)
    part = None
    for copy in band_copies:
        copy.wait()
    for at in CHUNKS:
        hi, lo = split(band[at, :])
        col_t[at, :] = mm(hi, hot_rows) + mm(lo, hot_rows)
        term = mm(hot[:, at], hi) + mm(hot[:, at], lo)
        part = term if part is None else part + term
    row_t[...] = part.T
    last = col_t[pl.ds(3, TILES * LOCI, stride=Q), :]
    for a in range(3):
        diff = col_t[pl.ds(a, TILES * LOCI, stride=Q), :] - last
        place = slice(a * LOCI, (a + 1) * LOCI)
        for e in range(DEPTH):
            core_ref[e, place, :] = diff[(2 * e + 1) * LOCI : (2 * e + 2) * LOCI]
            value = diff[(2 * e + 2) * LOCI : (2 * e + 3) * LOCI]
            if e == DEPTH - 1:
                value = jnp.where(dead, 0.0, value)
            mine_ref[e, place, :] = value
    for step in range(COLS):
        start = (col_at ^ step) * PIECE
        to = keep_ref if step < NEAR else give_ref
        last = row_t[pl.ds(start + 3, LOCI, stride=Q), :]
        for a in range(3):
            place = slice(a * LOCI, (a + 1) * LOCI)
            to[step % NEAR, place, :] = row_t[pl.ds(start + a, LOCI, stride=Q), :] - last


def first_slot(z):
    return lax.rem(z + 4, DEPTH)


def second_slot(z):
    return 7 - lax.rem(z, DEPTH)


def place_of():
    row_at = lax.axis_index("row")
    return row_at, lax.rem(row_at, 2) == 1, lax.rem(row_at // 2, DEPTH)


def combine_kernel(mine_ref, core_ref, z_ref, last_ref):
    _, odd, z_at = place_of()
    for d in range(DEPTH + 1):
        lower = core_ref[d] if d < DEPTH else jnp.zeros((SENT, BATCH), f32)
        upper = core_ref[d - 1] if d else jnp.zeros((SENT, BATCH), f32)
        value = jnp.where(odd, lower, upper)
        if d:
            value = value + mine_ref[d - 1]
        if d < DEPTH:
            z_ref[first_slot(z_at + d)] = value
        else:
            last_ref[...] = value


def add_kernel(keep_ref, got_ref, last_ref, *part_refs):
    del last_ref
    for step in range(NEAR):
        part_refs[step][...] = keep_ref[step] + got_ref[step]


def sum_kernel(z_ref, last_ref, hot_ref, hot_rows_ref, *rest):
    del hot_ref, hot_rows_ref
    row_refs, out_ref = rest[:NEAR], rest[NEAR]
    _, _, z_at = place_of()
    own = row_refs[0][...]
    for step in range(1, NEAR):
        own = own + row_refs[step][...]
    other = last_ref[...]
    for s in range(DEPTH):
        part = z_ref[FIRST.index(s)]
        own = own + jnp.where(s <= z_at, part, 0.0)
        other = other + jnp.where(s > z_at, part, 0.0)
    out_ref[:SENT, :] = own
    out_ref[SENT:, :] = other


def choose_kernel(z_ref, other_ref, core_ref):
    _, odd, z_at = place_of()
    for e in range(DEPTH):
        lower = z_ref[second_slot(z_at + e)]
        upper = z_ref[second_slot(z_at + e + 1)] if e < DEPTH - 1 else other_ref[...]
        core_ref[e] = jnp.where(odd, lower, upper)


def flip_kernel(hot_ref, hot_rows_ref, hot_t_ref, hot_rows_t_ref):
    eye = (iota((128, 128), 0) == iota((128, 128), 1)).astype(f32).astype(bf16)
    for j in range(9):
        at = slice(j * 128, min(BAND, (j + 1) * 128))
        turned = lax.dot_general(
            hot_ref[:, at], eye, (((0,), (0,)), ((), ())), preferred_element_type=f32
        )
        hot_t_ref[at, :] = turned.astype(bf16)
    turned = lax.dot_general(eye, hot_rows_ref[...], NT, preferred_element_type=f32)
    hot_rows_t_ref[...] = turned.astype(bf16)


def pair_kernel(own_ref, got_ref, out_ref):
    out_ref[0] = own_ref[...]
    out_ref[1] = got_ref[...]


def softmax_kernel(
    here_ref, there_ref, codes_ref, fields_ref, z_ref, row_ref, other_ref, new_fields_ref
):
    row_at = lax.axis_index("row")
    col_at = lax.axis_index("col")
    z_at = lax.rem(row_at // 2, DEPTH)
    lane = iota((LOCI, 128), 1)
    locus = iota((LOCI, 128), 0)
    start = col_at % 2 * PIECE
    own = []
    other = []
    columns = []
    for block in range(2):
        block_at = lax.rem(row_at + block * HALF, ROWS)
        line = fields_ref[pl.ds(block_at * 4 + col_at // 2, 1), :]
        columns = [
            jnp.sum(jnp.where(lane == start + locus * Q + a, line, 0.0), axis=1, keepdims=True)
            for a in range(Q)
        ]
        if block == 0:
            own_columns = columns
        diffs = []
        for a in range(3):
            here = here_ref[block * SENT + a * LOCI : block * SENT + (a + 1) * LOCI, :]
            flip = (1 - block) * SENT + a * LOCI
            there = there_ref[flip : flip + LOCI, :]
            diffs.append(here + there + (columns[a] - columns[3]))
        highest = jnp.maximum(jnp.maximum(diffs[0], diffs[1]), jnp.maximum(diffs[2], 0.0))
        expon = [jnp.exp(d - highest) for d in diffs]
        total = expon[0] + expon[1] + expon[2] + jnp.exp(-highest)
        codes = codes_ref[block]
        resid = [
            jnp.where(codes == float(a), 1.0, 0.0) - expon[a] / total for a in range(3)
        ]
        if block == 0:
            own = resid
        else:
            other = resid
    sums = [jnp.sum(x, axis=1, keepdims=True) for x in own]
    sums.append(-(sums[0] + sums[1] + sums[2]))
    line = jnp.zeros((LOCI, 128), f32)
    for a in range(Q):
        value = own_columns[a] + step_rate * (sums[a] / BATCH - field_decay * own_columns[a])
        line = line + jnp.where(lane == locus * Q + a, value, 0.0)
    new_fields_ref[...] = jnp.sum(line, axis=0, keepdims=True)
    for a in range(3):
        place = slice(a * LOCI, (a + 1) * LOCI)
        other_ref[place, :] = other[a]
        row_ref[place, :] = own[a]
        for s in range(DEPTH):
            z_ref[SECOND.index(s), place, :] = jnp.where(z_at >= s, own[a], other[a])


def fill(part, to_ref, at):
    pieces = [part[a * LOCI : (a + 1) * LOCI] for a in range(3)]
    pieces.append(-(pieces[0] + pieces[1] + pieces[2]))
    for a in range(Q):
        to_ref[pl.ds(at + a, LOCI, stride=Q), :] = pieces[a]


def masked(gradient, at):
    if at.start:
        return gradient
    col_at = lax.axis_index("col")
    spot = iota(gradient.shape, 0)
    same = (spot < PIECE) & ((col_at * PIECE + spot) // Q == iota(gradient.shape, 1) // Q)
    return jnp.where(same, 0.0, gradient)


def rows_kernel(band_ref, hot_cols_ref, *rest):
    row_refs, (out_ref, rows) = rest[:NEAR], rest[NEAR:]
    col_at = lax.axis_index("col")
    for step in range(COLS):
        fill(row_refs[step % NEAR][step // NEAR], rows, (col_at ^ step) * PIECE)
    rows_hi, rows_lo = split(rows[...].T)
    right = jnp.concatenate([rows_hi, rows_lo], axis=0)
    for at in CHUNKS:
        hot = hot_cols_ref[at, :]
        gradient = masked(mm(jnp.concatenate([hot, hot], axis=1), right), at)
        band = band_ref[at, :]
        out_ref[at, :] = band + step_rate * (gradient / BATCH - coupling_decay * band)


def cols_kernel(part_ref, z_ref, other_ref, core_ref, hot_rows_ref, out_ref, cols, new_ref, sems):
    row_at = lax.axis_index("row")
    z_at = lax.rem(row_at // 2, DEPTH)
    for j in range(TILES):
        if j % 2:
            part = core_ref[j // 2]
        elif j < HALF:
            part = z_ref[second_slot(z_at + j // 2)]
        else:
            part = other_ref[...]
        fill(part, cols, j * PIECE)
    hot_rows = hot_rows_ref[...]
    right = jnp.concatenate([hot_rows, hot_rows], axis=0)
    dead = row_at >= HALF
    copies = []
    for chunk, at in enumerate(CHUNKS):
        gradient = masked(mm(jnp.concatenate(split(cols[at, :]), axis=1), right), at)
        new = part_ref[at, :] + step_rate * (gradient / BATCH)
        if chunk == len(CHUNKS) - 1:
            spot = iota(new.shape, 0) + at.start
            new = jnp.where(dead & (spot >= HALF * PIECE), 0.0, new)
        new_ref[at, :] = new
        copies.append(pltpu.make_async_copy(new_ref.at[at], out_ref.at[at], sems.at[chunk]))
        copies[-1].start()
    for copy in copies:
        copy.wait()


COST = pl.CostEstimate(flops=4 * 10**10, bytes_accessed=10**6, transcendentals=0)


def call(kernel, outs, scratch=(), name=None, hbm=False, hbm_out=False, cost=None, loose=(), inputs=0):
    specs = {"in_specs": [pl.BlockSpec(memory_space=pltpu.HBM)] * 2} if hbm else {}
    if loose:
        specs["in_specs"] = [
            pl.BlockSpec(memory_space=pl.ANY if i in loose else pltpu.VMEM) for i in range(inputs)
        ]
    if hbm_out:
        specs["out_specs"] = pl.BlockSpec(memory_space=pltpu.HBM)
    return pl.pallas_call(
        kernel,
        out_shape=outs,
        scratch_shapes=list(scratch),
        compiler_params=pltpu.CompilerParams(
            vmem_limit_bytes=(52 if hbm else 24) * 1024 * 1024
        ),
        name=name,
        cost_estimate=cost,
        **specs,
    )


def arr(*shape, dtype=f32):
    return jax.ShapeDtypeStruct(shape, dtype)


def shards(seqs, fields, band):
    band_t = band.T
    piece = arr(SENT, BATCH)
    four = arr(NEAR, SENT, BATCH)
    eight = arr(DEPTH, SENT, BATCH)
    codes, mine, core, keep, give, hot, hot_rows = call(
        logits_kernel,
        (
            arr(2, LOCI, BATCH),
            eight,
            eight,
            four,
            four,
            arr(BATCH, 9 * 128, dtype=bf16),
            arr(SPAN, BATCH, dtype=bf16),
        ),
        [
            pltpu.VMEM((TILES, BATCH, 128), jnp.int32),
            pltpu.VMEM((BAND, SPAN), f32),
            pltpu.VMEM((SPAN, BATCH), f32),
            pltpu.VMEM((BAND, BATCH), f32),
            pltpu.SemaphoreType.DMA((TILES,)),
            pltpu.SemaphoreType.DMA((len(CHUNKS),)),
        ],
        "logit_parts",
        hbm=True,
    )(seqs, band_t)
    core = lax.ppermute(core, "row", SWAP_CORES)
    give = swap_cols(give, NEAR)
    z_send, last = call(combine_kernel, (eight, piece), name="combine")(mine, core)
    parts = call(add_kernel, (piece,) * NEAR, name="add_halves", cost=COST, loose=(2,), inputs=3)(
        keep, give, last
    )
    z_got = z_exchange(z_send, FIRST)
    row_got = [swap_cols(parts[step], step) for step in (3, 2, 1)] + [parts[0]]
    hot_cols, hot_rows = call(
        flip_kernel, (arr(BAND, BATCH, dtype=bf16), arr(BATCH, SPAN, dtype=bf16)), name="flip"
    )(hot, hot_rows)
    here = call(sum_kernel, arr(2 * SENT, BATCH), name="sum_parts", loose=(2, 3), inputs=8)(
        z_got, last, hot_cols, hot_rows, *row_got
    )
    there = lax.ppermute(here, "row", SWAP_HALVES)
    z_send, resid, other, new_fields = call(
        softmax_kernel,
        (eight, piece, piece, arr(1, 128)),
        name="softmax",
    )(here, there, codes, fields.reshape(-1, 128))
    across = swap_cols(resid, NEAR)
    z_all = z_exchange(z_send, SECOND)
    pair = call(pair_kernel, arr(2, SENT, BATCH), name="pair", cost=COST)(resid, across)
    row_all = [pair] + [swap_cols(pair, step) for step in range(1, NEAR)]
    core_all = lax.ppermute(
        call(choose_kernel, eight, name="choose")(z_all, other), "row", SWAP_CORES
    )
    part = call(
        rows_kernel, arr(BAND, SPAN), [pltpu.VMEM((SPAN, BATCH), f32)], "update_rows"
    )(band_t, hot_cols, *row_all)
    new_band_t = call(
        cols_kernel,
        arr(BAND, SPAN),
        [
            pltpu.VMEM((BAND, BATCH), f32),
            pltpu.VMEM((BAND, SPAN), f32),
            pltpu.SemaphoreType.DMA((len(CHUNKS),)),
        ],
        "update_cols",
        hbm_out=True,
    )(part, z_all, other, core_all, hot_rows)
    return new_band_t.T, new_fields[0, :PIECE]


def solution(mesh):
    in_specs = (P(), P(), P("row", "col"))
    out_specs = (P("row", "col"), P(("row", "col")))
    return jax.shard_map(shards, mesh=mesh, in_specs=in_specs, out_specs=out_specs, check_vma=False)
```
